32 devices in a mesh: label: 8 (over z, y), dp: 4 (over x, core).
Axes of the slice: x: 2, y: 2, z: 4, core: 2. Of those that a mesh axis runs over, the one named last changes fastest.
Arguments:
- queries: bfloat16 [4096, 768], P(('label', 'dp')), may hold values from -320 to 320
- weights: bfloat16 [5120, 768], P('label'), may hold values from -0.21875 to 0.21875
- counts: int32 [5120], P('label'), may hold values from 1 to 4096
- hits: int32 [4096, 4], P(('label', 'dp')), may hold values from 0 to 7, all different within a row; in each aligned block of 128 rows (0 to 127, 128 to 255, ...) at most 96 rows name the same one
- positive_offset: int32 [4096], P(('label', 'dp')), may hold values from 0 to 639
- cluster_shard: int32 [8], replicated, may hold values from 0 to 7, each once
Outputs:
- query_loss: float32 [4096], P(('label', 'dp'))
- query_grad: bfloat16 [4096, 768], P(('label', 'dp'))
- weight_grad: bfloat16 [5120, 768], P(('label', 'dp'))
The draws below stay inside these ranges and needn't reach their ends.
Inputs may be any that keep to these rules, and one draw needn't show every extreme that they name: `hits`: each query names 4 different clusters; the 128 queries of one device name any cluster at most 96 times, a bound that some block reaches. `cluster_shard`: each shard holds exactly one cluster.
All inputs are finite; a program needn't handle non-finite values.
Results may differ from the reference program's by a relative error of at most 0.0051.
Values may be sent and summed in bfloat16 or wider, within the bound.
No kernel may reach another device: no remote copies, remote signals or barrier semaphores. Data moves between devices by JAX's collectives and lax.ppermute only.
A program may use at most 64 MiB of HBM per device.

```python
import math
import jax
import jax.numpy as jnp
import numpy as np
from jax import lax

D = 768
LAB_DEV = 640
QROWS_DEV = 128
TOP = 4
SLOT_DEPTH = 96
CLUSTERS = 8
QUERIES = 4096
LABELS = 5120
N_LABEL = 8
N_DP = 4


def draw_queries(key, part):
    key = jax.random.fold_in(key, 11)
    base_key = jax.random.fold_in(key, 0)
    values = jax.random.normal(base_key, (QUERIES, D), jnp.float32)
    values = jnp.clip(values, -6.0, 6.0)
    return values.astype(jnp.bfloat16)


def touch_ends(entries, rng, low, largest):
    dims = entries.shape
    place = [jax.random.randint(jax.random.fold_in(rng, axis), (), 0, dims[axis]) for axis in range(len(dims))]
    entries = entries.at[tuple(place)].set(low)
    longest = dims.index(max(dims))
    place[longest] = (place[longest] + 1) % dims[longest]
    return entries.at[tuple(place)].set(largest)


def levels(own_key, dims, cuts, smallest, top_value):
    def one(dim, parts):
        draws = jax.random.uniform(jax.random.fold_in(jax.random.fold_in(own_key, 6), dim), (parts,), jnp.float32, smallest / len(cuts), top_value / len(cuts))
        return jnp.repeat(jnp.exp(draws), dims[dim] // parts).reshape((-1,) + (1,) * (len(dims) - dim - 1))

    level = one(*cuts[0])
    for cut in cuts[1:]:
        level = level * one(*cut)
    return level


def assign_block(stream_key, own, number, rows, amount, top, limit, lean):
    ranking = jax.random.permutation(stream_key, amount)
    crowded, common = portions_of(amount, rows * top, limit, lean, True), portions_of(amount, rows * top, limit, lean, False)
    places = jnp.arange(amount)

    def named(lengths, turn):
        used = int((lengths > 0).sum())
        fixed = max(1, used // 4)
        passed = fixed + (places - fixed + turn * (used - fixed)) % max(1, amount - fixed)
        return jnp.zeros((amount,), jnp.int32).at[ranking[jnp.where(places < fixed, places, passed)]].set(jnp.asarray(lengths, jnp.int32))

    lengths = jnp.where(number % 4 == 0, named(crowded, number // 4), named(common, number - number // 4 - 1))
    mixed = jax.random.permutation(jax.random.fold_in(own, 3), amount)
    donor, taker = mixed[0:amount // 2 * 2:2], mixed[1:amount // 2 * 2:2]
    slack = jnp.minimum(lengths[donor] - 1, limit - lengths[taker]) // 2
    slack = jnp.where((donor == ranking[0]) | (taker == ranking[0]) | (lengths[taker] == 0), 0, jnp.maximum(slack, 0))
    passed = jax.random.randint(jax.random.fold_in(own, 4), (amount // 2,), 0, 1 << 20) % (slack + 1)
    lengths = lengths.at[donor].add(-passed).at[taker].add(passed)
    items = jnp.searchsorted(jnp.cumsum(lengths), jnp.arange(rows * top), side="right").astype(jnp.int32)
    table = items.reshape(top, rows).T
    table = table[jax.random.permutation(jax.random.fold_in(own, 1), rows)]
    turn = jax.random.randint(jax.random.fold_in(own, 2), (rows, 1), 0, top)
    return jnp.take_along_axis(table, (jnp.arange(top)[None, :] + turn) % top, axis=1)


def portions_of(number_of, total, limit, skew, full):
    weights = [(1 << 20) // math.isqrt(rank ** skew) + 1 for rank in range(1, number_of + 1)]
    largest = limit if full else min(limit, max(-(-total // number_of), total * weights[0] // sum(weights)))
    least = 1 if total - largest >= number_of - 1 else 0
    given, rest = [largest] + [least] * (number_of - 1), total - largest - least * (number_of - 1)
    while rest > 0:
        free = [i for i in range(1, number_of) if given[i] < largest] or [i for i in range(1, number_of) if given[i] < limit]
        mass, remaining = sum([weights[i] for i in free]), rest
        for i in free:
            extra = min(limit - given[i], max(1, remaining * weights[i] // mass), rest)
            given[i] = given[i] + extra
            rest = rest - extra
    return np.array(given)


def normal_values(key, shape, width, most, pieces=(), held_as=jnp.bfloat16):
    gain = levels(key, shape, pieces, -0.22, 0.18) if pieces else 1.0
    entries = jax.random.normal(key, shape, jnp.float32) * width * gain
    return jnp.minimum(jnp.maximum(entries, -most), most).astype(held_as)


def setup_inputs(seed: int = 0) -> dict:
    key_of = jax.random.split(jax.random.key(seed), 7)
    queries = draw_queries(jax.random.fold_in(key_of[6], 71), 0)
    weights = normal_values(key_of[1], (LABELS, D), D ** -0.5, 0.21875, ((0, 8),))
    counts = touch_ends(jax.random.randint(key_of[2], (LABELS,), 1, 4097), jax.random.fold_in(key_of[2], 1), 1, 4096).astype(jnp.int32)
    hits_keys = jax.random.split(jax.random.fold_in(key_of[3], 1), QUERIES // QROWS_DEV)
    hits_turns = jax.random.permutation(jax.random.fold_in(key_of[3], 3), QUERIES // QROWS_DEV)
    hits = jax.vmap(lambda own, number: assign_block(jax.random.fold_in(key_of[3], 2), own, number, QROWS_DEV, CLUSTERS, TOP, SLOT_DEPTH, 2))(hits_keys, hits_turns).reshape((QUERIES, TOP))
    positive_offset = touch_ends(jax.random.randint(key_of[4], (QUERIES,), 0, LAB_DEV), jax.random.fold_in(key_of[4], 1), 0, LAB_DEV - 1).astype(jnp.int32)
    cluster_shard = jax.random.permutation(key_of[5], CLUSTERS).astype(jnp.int32)
    return dict(queries=queries, weights=weights, counts=counts, hits=hits, positive_offset=positive_offset, cluster_shard=cluster_shard)


def routing(hits, cluster_shard):
    owner_shard = cluster_shard[hits].reshape(N_LABEL, N_DP, QROWS_DEV * TOP).astype(jnp.int32)
    owner_table = (owner_shard[..., None] == jnp.arange(N_LABEL, dtype=jnp.int32)).astype(jnp.int32)
    position = jnp.sum((jnp.cumsum(owner_table, axis=2) - owner_table) * owner_table, axis=3)
    return owner_shard, position.astype(jnp.int32)


def slot_queries(query_grid, holder_row):
    slot_total = N_LABEL * SLOT_DEPTH
    source_index = jnp.arange(slot_total, dtype=jnp.int32) // SLOT_DEPTH
    group_index = jnp.arange(N_DP, dtype=jnp.int32)[:, None]
    valid_slot = holder_row >= 0
    slot_entry = jnp.maximum(holder_row, 0)
    picked = query_grid[source_index[None, :], group_index, slot_entry // TOP]
    picked = jnp.where(valid_slot[..., None], picked, jnp.zeros_like(picked))
    return picked, valid_slot, slot_entry, source_index


def slot_scores(picked, weight_block, log_block):
    products = jnp.einsum("gsd,ld->gsl", picked.astype(jnp.float32), weight_block.astype(jnp.float32))
    return products - log_block[None, None, :]


def reference(queries, weights, counts, hits, positive_offset, cluster_shard):
    query_grid = queries.reshape(N_LABEL, N_DP, QROWS_DEV, D)
    offset_grid = positive_offset.reshape(N_LABEL, N_DP, QROWS_DEV)
    weight_blocks = weights.reshape(N_LABEL, LAB_DEV, D)
    log_blocks = jnp.log(counts.astype(jnp.float32)).reshape(N_LABEL, LAB_DEV)
    owner_shard, position = routing(hits, cluster_shard)
    entry_total = QROWS_DEV * TOP
    source_grid = jnp.broadcast_to(jnp.arange(N_LABEL, dtype=jnp.int32)[:, None, None], owner_shard.shape)
    group_grid = jnp.broadcast_to(jnp.arange(N_DP, dtype=jnp.int32)[None, :, None], owner_shard.shape)
    entry_grid = jnp.broadcast_to(jnp.arange(entry_total, dtype=jnp.int32)[None, None, :], owner_shard.shape)
    slot_grid = source_grid * SLOT_DEPTH + position
    holder = jnp.full((N_LABEL, N_DP, N_LABEL * SLOT_DEPTH), -1, jnp.int32)
    holder = holder.at[owner_shard, group_grid, slot_grid].set(entry_grid)

    def first_pass(inputs):
        holder_row, weight_block, log_block = inputs
        picked, valid_slot, slot_entry, source_index = slot_queries(query_grid, holder_row)
        scores = slot_scores(picked, weight_block, log_block)
        local_max = jnp.max(scores, axis=2)
        local_sum = jnp.sum(jnp.exp(scores - local_max[..., None]), axis=2)
        return local_max, local_sum

    stat_max, stat_sum = lax.map(first_pass, (holder, weight_blocks, log_blocks))
    each_max = stat_max[owner_shard, group_grid, slot_grid].reshape(N_LABEL, N_DP, QROWS_DEV, TOP)
    each_sum = stat_sum[owner_shard, group_grid, slot_grid].reshape(N_LABEL, N_DP, QROWS_DEV, TOP)
    row_peak = jnp.max(each_max, axis=3)
    normal = row_peak + jnp.log(jnp.sum(each_sum * jnp.exp(each_max - row_peak[..., None]), axis=3))

    def second_pass(carry, inputs):
        holder_row, weight_block, log_block = inputs
        picked, valid_slot, slot_entry, source_index = slot_queries(query_grid, holder_row)
        scores = slot_scores(picked, weight_block, log_block)
        group_index = jnp.arange(N_DP, dtype=jnp.int32)[:, None]
        row_index = slot_entry // TOP
        slot_normal = jnp.where(valid_slot, normal[source_index[None, :], group_index, row_index], 0.0)
        target = jnp.where(valid_slot & (slot_entry % TOP == 0), offset_grid[source_index[None, :], group_index, row_index], -1)
        hit_label = jnp.arange(LAB_DEV, dtype=jnp.int32)[None, None, :] == target[..., None]
        coefficient = (jnp.exp(scores - slot_normal[..., None]) - hit_label.astype(jnp.float32)).astype(jnp.bfloat16)
        positive_score = jnp.sum(jnp.where(hit_label, scores, 0.0), axis=2).astype(jnp.bfloat16)
        slot_grad = jnp.einsum("gsl,ld->gsd", coefficient.astype(jnp.float32), weight_block.astype(jnp.float32)).astype(jnp.bfloat16)
        block_grad = jnp.einsum("gsl,gsd->ld", coefficient.astype(jnp.float32), picked.astype(jnp.float32)).astype(jnp.bfloat16)
        target_row = jnp.where(valid_slot, row_index, QROWS_DEV)
        source_full = jnp.broadcast_to(source_index[None, :], target_row.shape)
        group_full = jnp.broadcast_to(group_index, target_row.shape)
        carry = carry.at[source_full, group_full, target_row].add(slot_grad.astype(jnp.float32), mode="drop")
        return carry, (block_grad, positive_score)

    start_grad = jnp.zeros((N_LABEL, N_DP, QROWS_DEV, D), jnp.float32)
    query_grad, (weight_grad, positive_all) = lax.scan(second_pass, start_grad, (holder, weight_blocks, log_blocks))
    positive_entry = positive_all[owner_shard, group_grid, slot_grid].reshape(N_LABEL, N_DP, QROWS_DEV, TOP)[..., 0]
    query_loss = normal - positive_entry.astype(jnp.float32)
    return (query_loss.reshape(QUERIES), query_grad.astype(jnp.bfloat16).reshape(QUERIES, D), weight_grad.reshape(LABELS, D))
```

```python
import jax
import jax.numpy as jnp
from jax import lax
from jax.sharding import PartitionSpec as P

exact = lax.Precision.HIGHEST
LOW = -1e30


def from_slots(values, picker):
    return jnp.dot(picker, values, precision=exact)


def to_slots(values, picker):
    return jnp.dot(values, picker, precision=exact)


def slot_plan(queries, weights, counts, hits, positive_offset, cluster_shard):
    peer_count = lax.axis_size("label")
    row_count, top_count = hits.shape
    slot_count = 3 * row_count * top_count // 2
    slot_depth = slot_count // peer_count
    cluster_count = cluster_shard.shape[0]
    hit_flat = hits.reshape(-1)
    match_table = hit_flat[:, None] == jnp.arange(cluster_count, dtype=jnp.int32)[None, :]
    target_shard = jnp.sum(jnp.where(match_table, cluster_shard[None, :], 0), axis=1)
    owner_table = (
        target_shard[:, None] == jnp.arange(peer_count, dtype=jnp.int32)[None, :]
    ).astype(jnp.int32)
    position = jnp.sum((jnp.cumsum(owner_table, axis=0) - owner_table) * owner_table, axis=1)
    slot_of = target_shard * slot_depth + position
    picker_bool = slot_of[:, None] == jnp.arange(slot_count, dtype=jnp.int32)[None, :]
    picker = picker_bool.astype(jnp.float32)
    dispatch = jnp.sum(picker_bool.reshape(row_count, top_count, slot_count), axis=1).astype(
        jnp.bfloat16
    )
    outgoing = lax.dot_general(
        dispatch, queries, (((0,), (0,)), ((), ())), preferred_element_type=jnp.float32
    ).astype(jnp.bfloat16)
    arrived = lax.all_to_all(outgoing, "label", split_axis=0, concat_axis=0, tiled=True)
    log_count = jnp.log(counts.astype(jnp.float32))
    scores = (
        lax.dot_general(
            arrived, weights, (((1,), (1,)), ((), ())), preferred_element_type=jnp.float32
        )
        - log_count[None, :]
    )
    local_max = jnp.max(scores, axis=1)
    back_max = lax.all_to_all(local_max, "label", split_axis=0, concat_axis=0, tiled=True)
    row_peak = jnp.max(from_slots(back_max, picker).reshape(row_count, top_count), axis=1)
    peak_slots = to_slots(jnp.repeat(row_peak, top_count), picker)
    peak_here = lax.all_to_all(peak_slots, "label", split_axis=0, concat_axis=0, tiled=True)
    local_sum = jnp.sum(jnp.exp(scores - peak_here[:, None]), axis=1)
    back_sum = lax.all_to_all(local_sum, "label", split_axis=0, concat_axis=0, tiled=True)
    exp_total = jnp.sum(from_slots(back_sum, picker).reshape(row_count, top_count), axis=1)
    normal = row_peak + jnp.log(exp_total)
    first_hit = jnp.arange(row_count * top_count, dtype=jnp.int32) % top_count == 0
    target_entry = jnp.where(first_hit, jnp.repeat(positive_offset, top_count) + 1, 0).astype(
        jnp.float32
    )
    norm_slots = to_slots(jnp.repeat(normal, top_count), picker)
    target_slots = to_slots(target_entry, picker)
    norm_here, target_here = (
        lax.all_to_all(norm_slots, "label", split_axis=0, concat_axis=0, tiled=True),
        lax.all_to_all(target_slots, "label", split_axis=0, concat_axis=0, tiled=True),
    )
    label_count = weights.shape[0]
    hit_label = jnp.arange(label_count, dtype=jnp.float32)[None, :] + 1.0 == target_here[:, None]
    probability = jnp.exp(scores - norm_here[:, None])
    coefficient = (probability - hit_label.astype(jnp.float32)).astype(jnp.bfloat16)
    positive_score = jnp.sum(jnp.where(hit_label, scores, 0.0), axis=1).astype(jnp.bfloat16)
    slot_grad = jnp.dot(coefficient, weights, preferred_element_type=jnp.float32).astype(
        jnp.bfloat16
    )
    back_grad, back_score = (
        lax.all_to_all(slot_grad, "label", split_axis=0, concat_axis=0, tiled=True),
        lax.all_to_all(positive_score, "label", split_axis=0, concat_axis=0, tiled=True),
    )
    query_grad = jnp.dot(dispatch, back_grad, preferred_element_type=jnp.float32).astype(
        jnp.bfloat16
    )
    entry_score = from_slots(back_score.astype(jnp.float32), picker).reshape(row_count, top_count)
    query_loss = normal - entry_score[:, 0]
    partial_sum = lax.dot_general(
        coefficient, arrived, (((0,), (0,)), ((), ())), preferred_element_type=jnp.float32
    )
    reduced = lax.psum_scatter(partial_sum, "dp", scatter_dimension=0, tiled=True)
    weight_grad = reduced.astype(jnp.bfloat16)
    return (query_loss, query_grad, weight_grad)


def dense_plan(queries, weights, counts, hits, positive_offset, cluster_shard):
    n = lax.axis_size("label")
    dp = lax.axis_size("dp")
    groups = n // 2
    rows, width = queries.shape
    labels = weights.shape[0]
    part = labels // dp
    me = lax.axis_index("label")
    lane = lax.axis_index("dp")

    def shift(x, k):
        return lax.ppermute(x, "label", [(i, (i + 2 * k) % n) for i in range(n)])

    def pair(x):
        return lax.ppermute(x, "label", [(i, i ^ 1) for i in range(n)])

    def core(x):
        return lax.ppermute(x, "dp", [(i, i ^ 1) for i in range(dp)])

    def side(x):
        return lax.ppermute(x, "dp", [(i, i ^ 2) for i in range(dp)])

    def corner(x):
        return lax.ppermute(
            x, ("label", "dp"), [(i * dp + j, (i ^ 1) * dp + (j ^ 2)) for i in range(n) for j in range(dp)]
        )

    query_blocks = [queries] + [shift(queries, k) for k in range(1, groups)]
    match = hits[:, :, None] == jnp.arange(cluster_shard.shape[0], dtype=jnp.int32)[None, None, :]
    owner = jnp.sum(jnp.where(match, cluster_shard[None, None, :], 0), axis=2)
    mask_bits = jnp.sum(jnp.left_shift(1, owner), axis=1)
    code = jnp.stack([mask_bits, owner[:, 0] * labels + positive_offset], 0)
    codes = [code] + [shift(code, k) for k in range(1, groups)]

    order = jnp.arange(dp, dtype=jnp.int32) ^ lane
    blocks = jnp.take(weights.reshape(dp, part, width), order, axis=0)
    near = blocks.reshape(2, 2, part, width)[:, 0].reshape(2 * part, width)
    far = blocks.reshape(2, 2, part, width)[:, 1].reshape(2 * part, width)
    near_pair = pair(near)
    far_pair = core(near_pair)
    held = jnp.concatenate([near, near_pair, far, far_pair], 0)
    log_own = jnp.log(counts.astype(jnp.float32))
    logs = [log_own, pair(log_own)]
    place = (order[:, None] * part + jnp.arange(part, dtype=jnp.int32)[None, :]).reshape(2, 2, part)
    logs = [jnp.take(v.reshape(dp, part), order, axis=0).reshape(2, 2, part) for v in logs]

    def arrange(a, b):
        return jnp.concatenate([a[:, 0].reshape(-1), b[:, 0].reshape(-1), a[:, 1].reshape(-1), b[:, 1].reshape(-1)])

    log_held = arrange(*logs)
    label_held = arrange(place + me * labels, place + (me ^ 1) * labels)
    shard_held = label_held // labels

    q = jnp.concatenate(query_blocks, 0)
    bits = jnp.concatenate([c[0] for c in codes])
    target = jnp.concatenate([c[1] for c in codes])
    named = (jnp.right_shift(bits[:, None], shard_held[None, :]) & 1) == 1
    hot = target[:, None] == label_held[None, :]
    scores = lax.dot_general(q, held, (((1,), (1,)), ((), ())), preferred_element_type=jnp.float32)
    scores = jnp.where(named, scores - log_held[None, :], LOW)
    peak = jnp.max(scores, axis=1)
    total = jnp.sum(jnp.where(named, jnp.exp(scores - peak[:, None]), 0.0), axis=1)
    positive = jnp.sum(jnp.where(hot, scores, 0.0), axis=1)

    stats = jnp.stack([peak, total, positive], 0).reshape(3, groups, rows)
    all_stats = [stats]
    for k in range(1, groups):
        got = shift(stats, k)
        all_stats.append(jnp.concatenate([got[:, groups - k :], got[:, : groups - k]], 1))
    all_stats = jnp.stack(all_stats, 0)
    row_peak = jnp.max(all_stats[:, 0], axis=0)
    normal = row_peak + jnp.log(
        jnp.sum(all_stats[:, 1] * jnp.exp(all_stats[:, 0] - row_peak[None]), axis=0)
    )
    positive_score = jnp.sum(all_stats[:, 2, 0], axis=0).astype(jnp.bfloat16).astype(jnp.float32)
    query_loss = normal[0] - positive_score

    probability = jnp.exp(scores - normal.reshape(-1)[:, None])
    coefficient = (probability - hot.astype(jnp.float32)).astype(jnp.bfloat16)
    weight_part = lax.dot_general(
        coefficient, q, (((0,), (0,)), ((), ())), preferred_element_type=jnp.float32
    )
    half = 4 * part
    arrived = core(weight_part[half:].astype(jnp.bfloat16))
    terms = jnp.dot(coefficient, held, preferred_element_type=jnp.float32).astype(jnp.bfloat16)
    terms = terms.reshape(groups, rows, width)
    grads = [terms[0]] + [shift(terms[k], groups - k) for k in range(1, groups)]
    summed = weight_part[:half] + arrived.astype(jnp.float32)
    own = summed[:part]
    sent = summed[part:].astype(jnp.bfloat16)
    other = [side(sent[:part]), pair(sent[part : 2 * part]), corner(sent[2 * part :])]
    weight_grad = (own + sum(o.astype(jnp.float32) for o in other)).astype(jnp.bfloat16)
    query_grad = sum(g.astype(jnp.float32) for g in grads).astype(jnp.bfloat16)
    return query_loss, query_grad, weight_grad


def solution(mesh):
    n, dp = mesh.shape["label"], mesh.shape["dp"]

    def local(queries, weights, counts, hits, positive_offset, cluster_shard):
        rows, top = hits.shape
        args = (queries, weights, counts, hits, positive_offset, cluster_shard)
        dense = n % 2 == 0 and dp == 4 and n <= 30 and (n // 2) * rows <= 3 * rows * top // 2
        return dense_plan(*args) if dense else slot_plan(*args)

    return jax.shard_map(
        local,
        mesh=mesh,
        in_specs=(
            P(("label", "dp"), None),
            P("label", None),
            P("label"),
            P(("label", "dp"), None),
            P(("label", "dp")),
            P(),
        ),
        out_specs=(P(("label", "dp")), P(("label", "dp"), None), P(("label", "dp"), None)),
        check_vma=False,
    )
```

```python
import functools

import jax
import jax.numpy as jnp
from jax import lax
from jax.experimental import pallas as pl
from jax.experimental.pallas import tpu as pltpu
from jax.sharding import PartitionSpec as P

exact = lax.Precision.HIGHEST
LOW = -1e30


def from_slots(values, picker):
    return jnp.dot(picker, values, precision=exact)


def to_slots(values, picker):
    return jnp.dot(values, picker, precision=exact)


def slot_plan(queries, weights, counts, hits, positive_offset, cluster_shard):
    peer_count = lax.axis_size("label")
    row_count, top_count = hits.shape
    slot_count = 3 * row_count * top_count // 2
    slot_depth = slot_count // peer_count
    cluster_count = cluster_shard.shape[0]
    hit_flat = hits.reshape(-1)
    match_table = hit_flat[:, None] == jnp.arange(cluster_count, dtype=jnp.int32)[None, :]
    target_shard = jnp.sum(jnp.where(match_table, cluster_shard[None, :], 0), axis=1)
    owner_table = (
        target_shard[:, None] == jnp.arange(peer_count, dtype=jnp.int32)[None, :]
    ).astype(jnp.int32)
    position = jnp.sum((jnp.cumsum(owner_table, axis=0) - owner_table) * owner_table, axis=1)
    slot_of = target_shard * slot_depth + position
    picker_bool = slot_of[:, None] == jnp.arange(slot_count, dtype=jnp.int32)[None, :]
    picker = picker_bool.astype(jnp.float32)
    dispatch = jnp.sum(picker_bool.reshape(row_count, top_count, slot_count), axis=1).astype(
        jnp.bfloat16
    )
    outgoing = lax.dot_general(
        dispatch, queries, (((0,), (0,)), ((), ())), preferred_element_type=jnp.float32
    ).astype(jnp.bfloat16)
    arrived = lax.all_to_all(outgoing, "label", split_axis=0, concat_axis=0, tiled=True)
    log_count = jnp.log(counts.astype(jnp.float32))
    scores = (
        lax.dot_general(
            arrived, weights, (((1,), (1,)), ((), ())), preferred_element_type=jnp.float32
        )
        - log_count[None, :]
    )
    local_max = jnp.max(scores, axis=1)
    back_max = lax.all_to_all(local_max, "label", split_axis=0, concat_axis=0, tiled=True)
    row_peak = jnp.max(from_slots(back_max, picker).reshape(row_count, top_count), axis=1)
    peak_slots = to_slots(jnp.repeat(row_peak, top_count), picker)
    peak_here = lax.all_to_all(peak_slots, "label", split_axis=0, concat_axis=0, tiled=True)
    local_sum = jnp.sum(jnp.exp(scores - peak_here[:, None]), axis=1)
    back_sum = lax.all_to_all(local_sum, "label", split_axis=0, concat_axis=0, tiled=True)
    exp_total = jnp.sum(from_slots(back_sum, picker).reshape(row_count, top_count), axis=1)
    normal = row_peak + jnp.log(exp_total)
    first_hit = jnp.arange(row_count * top_count, dtype=jnp.int32) % top_count == 0
    target_entry = jnp.where(first_hit, jnp.repeat(positive_offset, top_count) + 1, 0).astype(
        jnp.float32
    )
    norm_slots = to_slots(jnp.repeat(normal, top_count), picker)
    target_slots = to_slots(target_entry, picker)
    norm_here, target_here = (
        lax.all_to_all(norm_slots, "label", split_axis=0, concat_axis=0, tiled=True),
        lax.all_to_all(target_slots, "label", split_axis=0, concat_axis=0, tiled=True),
    )
    label_count = weights.shape[0]
    hit_label = jnp.arange(label_count, dtype=jnp.float32)[None, :] + 1.0 == target_here[:, None]
    probability = jnp.exp(scores - norm_here[:, None])
    coefficient = (probability - hit_label.astype(jnp.float32)).astype(jnp.bfloat16)
    positive_score = jnp.sum(jnp.where(hit_label, scores, 0.0), axis=1).astype(jnp.bfloat16)
    slot_grad = jnp.dot(coefficient, weights, preferred_element_type=jnp.float32).astype(
        jnp.bfloat16
    )
    back_grad, back_score = (
        lax.all_to_all(slot_grad, "label", split_axis=0, concat_axis=0, tiled=True),
        lax.all_to_all(positive_score, "label", split_axis=0, concat_axis=0, tiled=True),
    )
    query_grad = jnp.dot(dispatch, back_grad, preferred_element_type=jnp.float32).astype(
        jnp.bfloat16
    )
    entry_score = from_slots(back_score.astype(jnp.float32), picker).reshape(row_count, top_count)
    query_loss = normal - entry_score[:, 0]
    partial_sum = lax.dot_general(
        coefficient, arrived, (((0,), (0,)), ((), ())), preferred_element_type=jnp.float32
    )
    reduced = lax.psum_scatter(partial_sum, "dp", scatter_dimension=0, tiled=True)
    weight_grad = reduced.astype(jnp.bfloat16)
    return (query_loss, query_grad, weight_grad)


FAR = 1e30
NT = (((1,), (1,)), ((), ()))
TN = (((0,), (0,)), ((), ()))
ROOM = pltpu.CompilerParams(vmem_limit_bytes=48 * 1024 * 1024)


def score(held, q, logs, s_ref):
    quarter = held.shape[0] // 4
    peaks = []
    for c in range(4):
        rows = pl.ds(c * quarter, quarter)
        s = lax.dot_general(held[rows, :], q, NT, preferred_element_type=jnp.float32) - logs[rows, :]
        s_ref[rows, :] = s
        peaks.append(jnp.max(s, axis=0, keepdims=True))
    peaks = [jnp.maximum(peaks[0], peaks[2]), jnp.maximum(peaks[1], peaks[3])]
    totals = []
    for c in range(4):
        e = jnp.exp(s_ref[pl.ds(c * quarter, quarter), :] - peaks[c % 2])
        totals.append(jnp.sum(e, axis=0, keepdims=True))
    return peaks[0], totals[0] + totals[2], peaks[1], totals[1] + totals[3]


def first_scores(qa, qb, near, near_pair, far, far_pair, logs, held, q, s_ref, stats):
    rows, quarter = qa.shape[0], near.shape[0]
    q[pl.ds(0, rows), :] = qa[...]
    q[pl.ds(rows, rows), :] = qb[...]
    for c, ref in enumerate((near, near_pair, far, far_pair)):
        held[pl.ds(c * quarter, quarter), :] = ref[pl.ds(0, quarter), :]
    for i, v in enumerate(score(held, q[...], logs, s_ref)):
        stats[2 * i : 2 * i + 1, :] = v[:, :rows]
        stats[2 * i + 1 : 2 * i + 2, :] = v[:, rows:]


def last_scores(qa, qb, held, logs, stats, meta, q, s_ref, message):
    rows = qa.shape[0]
    q[pl.ds(0, rows), :] = qa[...]
    q[pl.ds(rows, rows), :] = qb[...]
    for i, v in enumerate(score(held, q[...], logs, s_ref)):
        message[4 * i : 4 * i + 2, :] = stats[2 * i : 2 * i + 2, :]
        message[4 * i + 2 : 4 * i + 3, :] = v[:, :rows]
        message[4 * i + 3 : 4 * i + 4, :] = v[:, rows:]
    message[16:24, :] = meta[...]


def terms(blocks, labels, where, m0, m1, m2, m3, s_ref, held, coef, out_a, out_b, normals):
    messages = (m0, m1, m2, m3)
    me, lane = where[0], where[1]
    rows = m0.shape[1]
    part = labels // 4
    lines = {"normal": [], "near": [], "pair": [], "target": []}
    for j in blocks:
        bits = messages[j][16:17, :].astype(jnp.int32)
        pairs = []
        for k in range(4):
            for side in range(2):
                shard = (me ^ (2 * k)) ^ side
                named = (jnp.right_shift(bits, shard) & 1) == 1
                i = 8 * side + (j ^ k)
                pairs.append((named, messages[k][i : i + 1, :], messages[k][i + 4 : i + 5, :]))
        peak = functools.reduce(jnp.maximum, [jnp.where(n, m, LOW) for n, m, _ in pairs])
        total = sum(jnp.where(n, t * jnp.exp(jnp.where(n, m - peak, 0.0)), 0.0) for n, m, t in pairs)
        normal = peak + jnp.log(total)
        lines["normal"].append(normal)
        lines["near"].append(jnp.where(pairs[0][0], normal, FAR))
        lines["pair"].append(jnp.where(pairs[1][0], normal, FAR))
        lines["target"].append(messages[j][17:18, :].astype(jnp.int32))
    lines = {name: jnp.concatenate(v, 1) for name, v in lines.items()}
    normals[0:1, :] = lines["normal"][:, :rows]
    normals[1:2, :] = lines["normal"][:, rows:]
    index = lax.broadcasted_iota(jnp.int32, (part, 2 * rows), 0)
    positive = jnp.zeros((1, 2 * rows), jnp.float32)
    for c in range(4):
        side, core = c % 2, c // 2
        for x in range(2):
            at = pl.ds((2 * c + x) * part, part)
            base = (me ^ side) * labels + ((2 * x + core) ^ lane) * part
            s = s_ref[at, :]
            hot = index == lines["target"] - base
            p = jnp.exp(s - lines["pair" if side else "near"])
            coef[at, :] = (p - jnp.where(hot, 1.0, 0.0)).astype(jnp.bfloat16)
            positive += jnp.sum(jnp.where(hot, s, 0.0), axis=0, keepdims=True)
    grad = lax.dot_general(coef[...], held[...], TN, preferred_element_type=jnp.float32)
    grad = grad.astype(jnp.bfloat16)
    for i, out in enumerate((out_a, out_b)):
        out[pl.ds(0, rows), :] = grad[i * rows : (i + 1) * rows]
        line = positive[:, i * rows : (i + 1) * rows]
        line = jnp.broadcast_to(line, (16, rows)).astype(jnp.bfloat16)
        out[pl.ds(rows, 16), :] = jnp.zeros((16, out.shape[1]), jnp.bfloat16)
        out[pl.ds(rows, 16), pl.ds(0, rows)] = line


def label_terms(coef_a, coef_b, qa, qb, kept, sent):
    half = kept.shape[0]
    for i, out in enumerate((sent, kept)):
        at = pl.ds((1 - i) * half, half)
        out[...] = (
            jnp.dot(coef_a[at, :], qa[...], preferred_element_type=jnp.float32)
            + jnp.dot(coef_b[at, :], qb[...], preferred_element_type=jnp.float32)
        ).astype(out.dtype)


def dense_plan(queries, weights, counts, hits, positive_offset, cluster_shard):
    n = lax.axis_size("label")
    dp = lax.axis_size("dp")
    rows, width = queries.shape
    labels = weights.shape[0]
    part = labels // dp
    me = lax.axis_index("label")
    lane = lax.axis_index("dp")
    f32, bf16 = jnp.float32, jnp.bfloat16
    shape = jax.ShapeDtypeStruct

    def swap(x, k):
        return lax.ppermute(x, "label", [(i, i ^ (2 * k)) for i in range(n)])

    def pair(x):
        return lax.ppermute(x, "label", [(i, i ^ 1) for i in range(n)])

    def core(x):
        return lax.ppermute(x, "dp", [(i, i ^ 1) for i in range(dp)])

    def side(x):
        return lax.ppermute(x, "dp", [(i, i ^ 2) for i in range(dp)])

    def corner(x):
        return lax.ppermute(
            x, ("label", "dp"), [(i * dp + j, (i ^ 1) * dp + (j ^ 2)) for i in range(n) for j in range(dp)]
        )

    order = jnp.arange(dp, dtype=jnp.int32) ^ lane
    blocks = jnp.take(weights.reshape(dp, part, width), order, axis=0)
    blocks = blocks.reshape(2, 2, part, width)
    near = blocks[:, 0].reshape(2 * part, width)
    far = blocks[:, 1].reshape(2 * part, width)
    count = jnp.take(counts.reshape(dp, part), order, axis=0).reshape(2, 2, part)
    count_near, count_far = count[:, 0].reshape(-1), count[:, 1].reshape(-1)
    line = jnp.concatenate([count_near >> 6, count_near & 63, jnp.zeros((width - 4 * part,), jnp.int32)])
    line = jnp.pad(line.astype(bf16)[None, :], ((0, 15), (0, 0)))
    near_pair = pair(jnp.concatenate([near, line], 0))
    q2, q3, q1 = swap(queries, 2), swap(queries, 3), swap(queries, 1)
    far_pair = core(near_pair)

    def carried(x):
        digits = x[2 * part, : 4 * part].astype(jnp.int32)
        return digits[: 2 * part] * 64 + digits[2 * part :]

    count_held = jnp.concatenate([count_near, carried(near_pair), count_far, carried(far_pair)])
    logs = jnp.log(count_held.astype(f32))[:, None]

    match = hits[:, :, None] == jnp.arange(cluster_shard.shape[0], dtype=jnp.int32)[None, None, :]
    owner = jnp.sum(jnp.where(match, cluster_shard[None, None, :], 0), axis=2)
    bits = jnp.sum(jnp.left_shift(1, owner), axis=1)
    target = owner[:, 0] * labels + positive_offset
    meta = jnp.pad(jnp.stack([bits, target]).astype(f32), ((0, 6), (0, 0)))

    held, qa, sa, stats = pl.pallas_call(
        first_scores,
        out_shape=(
            shape((2 * labels, width), bf16),
            shape((2 * rows, width), bf16),
            shape((2 * labels, 2 * rows), f32),
            shape((8, rows), f32),
        ),
        compiler_params=ROOM,
        name="first_scores",
    )(queries, q1, near, near_pair, far, far_pair, logs)
    qb, sb, message = pl.pallas_call(
        last_scores,
        out_shape=(shape((2 * rows, width), bf16), shape((2 * labels, 2 * rows), f32), shape((24, rows), f32)),
        compiler_params=ROOM,
        name="last_scores",
    )(q2, q3, held, logs, stats, meta)

    m3, m2, m1 = swap(message, 3), swap(message, 2), swap(message, 1)
    where = jnp.stack([me, lane]).astype(jnp.int32)

    def gradient(pairing, s):
        spec = pl.BlockSpec(memory_space=pltpu.VMEM)
        return pl.pallas_call(
            functools.partial(terms, pairing, labels),
            out_shape=(
                shape((2 * labels, 2 * rows), bf16),
                shape((rows + 16, width), bf16),
                shape((rows + 16, width), bf16),
                shape((2, rows), f32),
            ),
            in_specs=[pl.BlockSpec(memory_space=pltpu.SMEM)] + [spec] * 6,
            compiler_params=ROOM,
            name="terms",
        )(where, message, m1, m2, m3, s, held)

    coef_b, t2, t3, _ = gradient((2, 3), sb)
    coef_a, t0, t1, normals = gradient((0, 1), sa)
    kept, sent = pl.pallas_call(
        label_terms,
        out_shape=(shape((labels, width), f32), shape((labels, width), bf16)),
        compiler_params=ROOM,
        name="label_terms",
    )(coef_a, coef_b, qa, qb)
    arrived = core(sent)
    g3, g2, g1 = swap(t3, 3), swap(t2, 2), swap(t1, 1)
    summed = kept + arrived.astype(f32)
    sent = summed[part:].astype(bf16)
    other = [side(sent[:part]), pair(sent[part : 2 * part]), corner(sent[2 * part :])]
    weight_grad = (summed[:part] + sum(o.astype(f32) for o in other)).astype(bf16)
    grads = sum(g.astype(f32) for g in (t0, g1, g2, g3))
    return normals[0] - grads[rows, :rows], grads[:rows].astype(bf16), weight_grad


def solution(mesh):
    n, dp = mesh.shape["label"], mesh.shape["dp"]

    def local(queries, weights, counts, hits, positive_offset, cluster_shard):
        rows, top = hits.shape
        args = (queries, weights, counts, hits, positive_offset, cluster_shard)
        dense = n == 8 and dp == 4 and (n // 2) * rows <= 3 * rows * top // 2
        return dense_plan(*args) if dense else slot_plan(*args)

    return jax.shard_map(
        local,
        mesh=mesh,
        in_specs=(
            P(("label", "dp"), None),
            P("label", None),
            P("label"),
            P(("label", "dp"), None),
            P(("label", "dp")),
            P(),
        ),
        out_specs=(P(("label", "dp")), P(("label", "dp"), None), P(("label", "dp"), None)),
        check_vma=False,
    )
```

```python
import functools

import jax
import jax.numpy as jnp
from jax import lax
from jax.experimental import pallas as pl
from jax.experimental.pallas import tpu as pltpu
from jax.sharding import PartitionSpec as P

exact = lax.Precision.HIGHEST
LOW = -1e30


def from_slots(values, picker):
    return jnp.dot(picker, values, precision=exact)


def to_slots(values, picker):
    return jnp.dot(values, picker, precision=exact)


def slot_plan(queries, weights, counts, hits, positive_offset, cluster_shard):
    peer_count = lax.axis_size("label")
    row_count, top_count = hits.shape
    slot_count = 3 * row_count * top_count // 2
    slot_depth = slot_count // peer_count
    cluster_count = cluster_shard.shape[0]
    hit_flat = hits.reshape(-1)
    match_table = hit_flat[:, None] == jnp.arange(cluster_count, dtype=jnp.int32)[None, :]
    target_shard = jnp.sum(jnp.where(match_table, cluster_shard[None, :], 0), axis=1)
    owner_table = (
        target_shard[:, None] == jnp.arange(peer_count, dtype=jnp.int32)[None, :]
    ).astype(jnp.int32)
    position = jnp.sum((jnp.cumsum(owner_table, axis=0) - owner_table) * owner_table, axis=1)
    slot_of = target_shard * slot_depth + position
    picker_bool = slot_of[:, None] == jnp.arange(slot_count, dtype=jnp.int32)[None, :]
    picker = picker_bool.astype(jnp.float32)
    dispatch = jnp.sum(picker_bool.reshape(row_count, top_count, slot_count), axis=1).astype(
        jnp.bfloat16
    )
    outgoing = lax.dot_general(
        dispatch, queries, (((0,), (0,)), ((), ())), preferred_element_type=jnp.float32
    ).astype(jnp.bfloat16)
    arrived = lax.all_to_all(outgoing, "label", split_axis=0, concat_axis=0, tiled=True)
    log_count = jnp.log(counts.astype(jnp.float32))
    scores = (
        lax.dot_general(
            arrived, weights, (((1,), (1,)), ((), ())), preferred_element_type=jnp.float32
        )
        - log_count[None, :]
    )
    local_max = jnp.max(scores, axis=1)
    back_max = lax.all_to_all(local_max, "label", split_axis=0, concat_axis=0, tiled=True)
    row_peak = jnp.max(from_slots(back_max, picker).reshape(row_count, top_count), axis=1)
    peak_slots = to_slots(jnp.repeat(row_peak, top_count), picker)
    peak_here = lax.all_to_all(peak_slots, "label", split_axis=0, concat_axis=0, tiled=True)
    local_sum = jnp.sum(jnp.exp(scores - peak_here[:, None]), axis=1)
    back_sum = lax.all_to_all(local_sum, "label", split_axis=0, concat_axis=0, tiled=True)
    exp_total = jnp.sum(from_slots(back_sum, picker).reshape(row_count, top_count), axis=1)
    normal = row_peak + jnp.log(exp_total)
    first_hit = jnp.arange(row_count * top_count, dtype=jnp.int32) % top_count == 0
    target_entry = jnp.where(first_hit, jnp.repeat(positive_offset, top_count) + 1, 0).astype(
        jnp.float32
    )
    norm_slots = to_slots(jnp.repeat(normal, top_count), picker)
    target_slots = to_slots(target_entry, picker)
    norm_here, target_here = (
        lax.all_to_all(norm_slots, "label", split_axis=0, concat_axis=0, tiled=True),
        lax.all_to_all(target_slots, "label", split_axis=0, concat_axis=0, tiled=True),
    )
    label_count = weights.shape[0]
    hit_label = jnp.arange(label_count, dtype=jnp.float32)[None, :] + 1.0 == target_here[:, None]
    probability = jnp.exp(scores - norm_here[:, None])
    coefficient = (probability - hit_label.astype(jnp.float32)).astype(jnp.bfloat16)
    positive_score = jnp.sum(jnp.where(hit_label, scores, 0.0), axis=1).astype(jnp.bfloat16)
    slot_grad = jnp.dot(coefficient, weights, preferred_element_type=jnp.float32).astype(
        jnp.bfloat16
    )
    back_grad, back_score = (
        lax.all_to_all(slot_grad, "label", split_axis=0, concat_axis=0, tiled=True),
        lax.all_to_all(positive_score, "label", split_axis=0, concat_axis=0, tiled=True),
    )
    query_grad = jnp.dot(dispatch, back_grad, preferred_element_type=jnp.float32).astype(
        jnp.bfloat16
    )
    entry_score = from_slots(back_score.astype(jnp.float32), picker).reshape(row_count, top_count)
    query_loss = normal - entry_score[:, 0]
    partial_sum = lax.dot_general(
        coefficient, arrived, (((0,), (0,)), ((), ())), preferred_element_type=jnp.float32
    )
    reduced = lax.psum_scatter(partial_sum, "dp", scatter_dimension=0, tiled=True)
    weight_grad = reduced.astype(jnp.bfloat16)
    return (query_loss, query_grad, weight_grad)


FAR = 1e30
NT = (((1,), (1,)), ((), ()))
TN = (((0,), (0,)), ((), ()))
ROOM = pltpu.CompilerParams(vmem_limit_bytes=20 * 1024 * 1024)


def cost(flops, size, exps=0):
    return pl.CostEstimate(flops=int(flops), bytes_accessed=int(size), transcendentals=int(exps))


def pack(where, weights, counts, out):
    lane = where[1]
    part = weights.shape[0] // 4
    for x in range(2):
        base = pl.multiple_of(((2 * x) ^ lane) * part, part)
        out[pl.ds(x * part, part), :] = weights[pl.ds(base, part), :]
    row = lax.broadcasted_iota(jnp.int32, (16, counts.shape[1]), 0)
    count = counts[...]
    high, low = jnp.right_shift(count, 6), count & 63
    digits = jnp.where(row == 0, high, jnp.where(row == 1, low, 0)).astype(jnp.float32)
    out[pl.ds(2 * part, 16), :] = jnp.zeros((16, out.shape[1]), jnp.bfloat16)
    out[pl.ds(2 * part, 16), pl.ds(0, counts.shape[1])] = digits.astype(jnp.bfloat16)


def score(held, q, logs, s_ref):
    quarter = held.shape[0] // 4
    peaks = []
    for c in range(4):
        rows = pl.ds(c * quarter, quarter)
        s = lax.dot_general(held[rows, :], q, NT, preferred_element_type=jnp.float32) - logs[rows, :]
        s_ref[rows, :] = s
        peaks.append(jnp.max(s, axis=0, keepdims=True))
    peaks = [jnp.maximum(peaks[0], peaks[2]), jnp.maximum(peaks[1], peaks[3])]
    totals = []
    for c in range(4):
        e = jnp.exp(s_ref[pl.ds(c * quarter, quarter), :] - peaks[c % 2])
        totals.append(jnp.sum(e, axis=0, keepdims=True))
    return peaks[0], totals[0] + totals[2], peaks[1], totals[1] + totals[3]


def first_scores(where, qa, qb, weights, counts, near_pair, far_pair, held, q, s_ref, stats, logs, column):
    lane = where[1]
    rows, labels = qa.shape[0], weights.shape[0]
    part, half = labels // 4, labels // 2
    q[pl.ds(0, rows), :] = qa[...]
    q[pl.ds(rows, rows), :] = qb[...]
    digits = near_pair[pl.ds(half, 16), :].astype(jnp.float32)[:, :labels]
    lines = (counts[...].astype(jnp.float32), digits[0:1] * 64.0 + digits[1:2])
    for side, line in enumerate(lines):
        column[...] = jnp.transpose(jnp.broadcast_to(jnp.log(line), (8, labels)))
        for core in range(2):
            for x in range(2):
                at = pl.ds((4 * core + 2 * side + x) * part, part)
                base = pl.multiple_of(((2 * x + core) ^ lane) * part, part)
                logs[at, :] = column[pl.ds(base, part), 0:1]
                if side:
                    held[at, :] = (far_pair if core else near_pair)[pl.ds(x * part, part), :]
                else:
                    held[at, :] = weights[pl.ds(base, part), :]
    for i, v in enumerate(score(held, q[...], logs, s_ref)):
        stats[2 * i : 2 * i + 1, :] = v[:, :rows]
        stats[2 * i + 1 : 2 * i + 2, :] = v[:, rows:]


def last_scores(qa, qb, held, logs, stats, meta, q, s_ref, message):
    rows = qa.shape[0]
    q[pl.ds(0, rows), :] = qa[...]
    q[pl.ds(rows, rows), :] = qb[...]
    for i, v in enumerate(score(held, q[...], logs, s_ref)):
        message[4 * i : 4 * i + 2, :] = stats[2 * i : 2 * i + 2, :]
        message[4 * i + 2 : 4 * i + 3, :] = v[:, :rows]
        message[4 * i + 3 : 4 * i + 4, :] = v[:, rows:]
    message[16:24, :] = meta[...]


def terms(blocks, labels, where, m0, m1, m2, m3, s_ref, held, coef, out_a, out_b, normals):
    messages = (m0, m1, m2, m3)
    me, lane = where[0], where[1]
    rows = m0.shape[1]
    part = labels // 4
    lines = {"normal": [], "near": [], "pair": [], "target": []}
    for j in blocks:
        bits = messages[j][16:17, :].astype(jnp.int32)
        pairs = []
        for k in range(4):
            for side in range(2):
                shard = (me ^ (2 * k)) ^ side
                named = (jnp.right_shift(bits, shard) & 1) == 1
                i = 8 * side + (j ^ k)
                pairs.append((named, messages[k][i : i + 1, :], messages[k][i + 4 : i + 5, :]))
        peak = functools.reduce(jnp.maximum, [jnp.where(n, m, LOW) for n, m, _ in pairs])
        total = sum(jnp.where(n, t * jnp.exp(jnp.where(n, m - peak, 0.0)), 0.0) for n, m, t in pairs)
        normal = peak + jnp.log(total)
        lines["normal"].append(normal)
        lines["near"].append(jnp.where(pairs[0][0], normal, FAR))
        lines["pair"].append(jnp.where(pairs[1][0], normal, FAR))
        lines["target"].append(messages[j][17:18, :].astype(jnp.int32))
    lines = {name: jnp.concatenate(v, 1) for name, v in lines.items()}
    normals[0:1, :] = lines["normal"][:, :rows]
    normals[1:2, :] = lines["normal"][:, rows:]
    index = lax.broadcasted_iota(jnp.int32, (part, 2 * rows), 0)
    positive = jnp.zeros((1, 2 * rows), jnp.float32)
    for c in range(4):
        side, core = c % 2, c // 2
        for x in range(2):
            at = pl.ds((2 * c + x) * part, part)
            base = (me ^ side) * labels + ((2 * x + core) ^ lane) * part
            s = s_ref[at, :]
            hot = index == lines["target"] - base
            p = jnp.exp(s - lines["pair" if side else "near"])
            coef[at, :] = (p - jnp.where(hot, 1.0, 0.0)).astype(jnp.bfloat16)
            positive += jnp.sum(jnp.where(hot, s, 0.0), axis=0, keepdims=True)
    grad = lax.dot_general(coef[...], held[...], TN, preferred_element_type=jnp.float32)
    grad = grad.astype(jnp.bfloat16)
    for i, out in enumerate((out_a, out_b)):
        out[pl.ds(0, rows), :] = grad[i * rows : (i + 1) * rows]
        line = positive[:, i * rows : (i + 1) * rows]
        line = jnp.broadcast_to(line, (16, rows)).astype(jnp.bfloat16)
        out[pl.ds(rows, 16), :] = jnp.zeros((16, out.shape[1]), jnp.bfloat16)
        out[pl.ds(rows, 16), pl.ds(0, rows)] = line


def label_terms(coef_a, coef_b, qa, qb, kept, sent):
    half = kept.shape[0]
    for i, out in enumerate((sent, kept)):
        at = pl.ds((1 - i) * half, half)
        out[...] = (
            jnp.dot(coef_a[at, :], qa[...], preferred_element_type=jnp.float32)
            + jnp.dot(coef_b[at, :], qb[...], preferred_element_type=jnp.float32)
        ).astype(out.dtype)


def finish(normals, t0, t1, t2, t3, own, s0, s1, s2, loss, query_grad, weight_grad):
    f32 = jnp.float32
    rows = query_grad.shape[0]
    total = sum(t[pl.ds(0, rows), :].astype(f32) for t in (t0, t1, t2, t3))
    query_grad[...] = total.astype(query_grad.dtype)
    line = sum(t[pl.ds(rows, 16), pl.ds(0, rows)].astype(f32) for t in (t0, t1, t2, t3))
    loss[...] = normals[0:1, :] - line[0:1]
    total = own[...] + sum(s[...].astype(f32) for s in (s0, s1, s2))
    weight_grad[...] = total.astype(weight_grad.dtype)


def dense_plan(queries, weights, counts, hits, positive_offset, cluster_shard):
    n = lax.axis_size("label")
    dp = lax.axis_size("dp")
    rows, width = queries.shape
    labels = weights.shape[0]
    part = labels // dp
    me = lax.axis_index("label")
    lane = lax.axis_index("dp")
    f32, bf16 = jnp.float32, jnp.bfloat16
    shape = jax.ShapeDtypeStruct

    def swap(x, k):
        return lax.ppermute(x, "label", [(i, i ^ (2 * k)) for i in range(n)])

    def pair(x):
        return lax.ppermute(x, "label", [(i, i ^ 1) for i in range(n)])

    def core(x):
        return lax.ppermute(x, "dp", [(i, i ^ 1) for i in range(dp)])

    def side(x):
        return lax.ppermute(x, "dp", [(i, i ^ 2) for i in range(dp)])

    def corner(x):
        return lax.ppermute(
            x, ("label", "dp"), [(i * dp + j, (i ^ 1) * dp + (j ^ 2)) for i in range(n) for j in range(dp)]
        )

    def specs(scalars, arrays):
        return [pl.BlockSpec(memory_space=pltpu.SMEM)] * scalars + [pl.BlockSpec(memory_space=pltpu.VMEM)] * arrays

    where = jnp.stack([me, lane]).astype(jnp.int32)
    count_line = counts.reshape(1, labels)
    packed = pl.pallas_call(
        pack,
        out_shape=shape((labels // 2 + 16, width), bf16),
        in_specs=specs(1, 2),
        cost_estimate=cost(0, labels * width * 3),
        compiler_params=ROOM,
        name="pack",
    )(where, weights, count_line)
    near_pair = pair(packed)
    q2, q3, q1 = swap(queries, 2), swap(queries, 3), swap(queries, 1)
    far_pair = core(near_pair)

    match = hits[:, :, None] == jnp.arange(cluster_shard.shape[0], dtype=jnp.int32)[None, None, :]
    owner = jnp.sum(jnp.where(match, cluster_shard[None, None, :], 0), axis=2)
    bits = jnp.sum(jnp.left_shift(1, owner), axis=1)
    target = owner[:, 0] * labels + positive_offset
    meta = jnp.pad(jnp.stack([bits, target]).astype(f32), ((0, 6), (0, 0)))

    block_flops = 2 * (2 * labels) * (2 * rows) * width
    score_cost = cost(block_flops, 2 * labels * (width * 2 + rows * 8), 4 * labels * rows)
    held, qa, sa, stats, logs = pl.pallas_call(
        first_scores,
        out_shape=(
            shape((2 * labels, width), bf16),
            shape((2 * rows, width), bf16),
            shape((2 * labels, 2 * rows), f32),
            shape((8, rows), f32),
            shape((2 * labels, 1), f32),
        ),
        in_specs=specs(1, 6),
        scratch_shapes=[pltpu.VMEM((labels, 8), f32)],
        cost_estimate=score_cost,
        compiler_params=ROOM,
        name="first_scores",
    )(where, queries, q1, weights, count_line, near_pair, far_pair)
    qb, sb, message = pl.pallas_call(
        last_scores,
        out_shape=(shape((2 * rows, width), bf16), shape((2 * labels, 2 * rows), f32), shape((24, rows), f32)),
        cost_estimate=score_cost,
        compiler_params=ROOM,
        name="last_scores",
    )(q2, q3, held, logs, stats, meta)

    m3, m2, m1 = swap(message, 3), swap(message, 2), swap(message, 1)

    def gradient(pairing, s):
        return pl.pallas_call(
            functools.partial(terms, pairing, labels),
            out_shape=(
                shape((2 * labels, 2 * rows), bf16),
                shape((rows + 16, width), bf16),
                shape((rows + 16, width), bf16),
                shape((2, rows), f32),
            ),
            in_specs=specs(1, 6),
            cost_estimate=score_cost,
            compiler_params=ROOM,
            name="terms",
        )(where, message, m1, m2, m3, s, held)

    coef_b, t2, t3, _ = gradient((2, 3), sb)
    coef_a, t0, t1, normals = gradient((0, 1), sa)
    kept, sent = pl.pallas_call(
        label_terms,
        out_shape=(shape((labels, width), f32), shape((labels, width), bf16)),
        cost_estimate=cost(2 * block_flops, labels * (width * 6 + rows * 16)),
        compiler_params=ROOM,
        name="label_terms",
    )(coef_a, coef_b, qa, qb)
    arrived = core(sent)
    g3, g2, g1 = swap(t3, 3), swap(t2, 2), swap(t1, 1)
    summed = kept + arrived.astype(f32)
    sent = summed[part:].astype(bf16)
    s0, s1, s2 = side(sent[:part]), pair(sent[part : 2 * part]), corner(sent[2 * part :])
    loss, query_grad, weight_grad = pl.pallas_call(
        finish,
        out_shape=(shape((1, rows), f32), shape((rows, width), bf16), shape((part, width), bf16)),
        cost_estimate=cost(0, 10 * rows * width + 10 * part * width),
        compiler_params=ROOM,
        name="finish",
    )(normals, t0, g1, g2, g3, summed[:part], s0, s1, s2)
    return loss[0], query_grad, weight_grad


def solution(mesh):
    n, dp = mesh.shape["label"], mesh.shape["dp"]

    def local(queries, weights, counts, hits, positive_offset, cluster_shard):
        rows, top = hits.shape
        args = (queries, weights, counts, hits, positive_offset, cluster_shard)
        dense = n == 8 and dp == 4 and (n // 2) * rows <= 3 * rows * top // 2
        return dense_plan(*args) if dense else slot_plan(*args)

    return jax.shard_map(
        local,
        mesh=mesh,
        in_specs=(
            P(("label", "dp"), None),
            P("label", None),
            P("label"),
            P(("label", "dp"), None),
            P(("label", "dp")),
            P(),
        ),
        out_specs=(P(("label", "dp")), P(("label", "dp"), None), P(("label", "dp"), None)),
        check_vma=False,
    )
```

```python
import functools

import jax
import jax.numpy as jnp
from jax import lax
from jax.experimental import pallas as pl
from jax.experimental.pallas import tpu as pltpu
from jax.sharding import PartitionSpec as P

exact = lax.Precision.HIGHEST
LOW = -1e30


def from_slots(values, picker):
    return jnp.dot(picker, values, precision=exact)


def to_slots(values, picker):
    return jnp.dot(values, picker, precision=exact)


def slot_plan(queries, weights, counts, hits, positive_offset, cluster_shard):
    peer_count = lax.axis_size("label")
    row_count, top_count = hits.shape
    slot_count = 3 * row_count * top_count // 2
    slot_depth = slot_count // peer_count
    cluster_count = cluster_shard.shape[0]
    hit_flat = hits.reshape(-1)
    match_table = hit_flat[:, None] == jnp.arange(cluster_count, dtype=jnp.int32)[None, :]
    target_shard = jnp.sum(jnp.where(match_table, cluster_shard[None, :], 0), axis=1)
    owner_table = (
        target_shard[:, None] == jnp.arange(peer_count, dtype=jnp.int32)[None, :]
    ).astype(jnp.int32)
    position = jnp.sum((jnp.cumsum(owner_table, axis=0) - owner_table) * owner_table, axis=1)
    slot_of = target_shard * slot_depth + position
    picker_bool = slot_of[:, None] == jnp.arange(slot_count, dtype=jnp.int32)[None, :]
    picker = picker_bool.astype(jnp.float32)
    dispatch = jnp.sum(picker_bool.reshape(row_count, top_count, slot_count), axis=1).astype(
        jnp.bfloat16
    )
    outgoing = lax.dot_general(
        dispatch, queries, (((0,), (0,)), ((), ())), preferred_element_type=jnp.float32
    ).astype(jnp.bfloat16)
    arrived = lax.all_to_all(outgoing, "label", split_axis=0, concat_axis=0, tiled=True)
    log_count = jnp.log(counts.astype(jnp.float32))
    scores = (
        lax.dot_general(
            arrived, weights, (((1,), (1,)), ((), ())), preferred_element_type=jnp.float32
        )
        - log_count[None, :]
    )
    local_max = jnp.max(scores, axis=1)
    back_max = lax.all_to_all(local_max, "label", split_axis=0, concat_axis=0, tiled=True)
    row_peak = jnp.max(from_slots(back_max, picker).reshape(row_count, top_count), axis=1)
    peak_slots = to_slots(jnp.repeat(row_peak, top_count), picker)
    peak_here = lax.all_to_all(peak_slots, "label", split_axis=0, concat_axis=0, tiled=True)
    local_sum = jnp.sum(jnp.exp(scores - peak_here[:, None]), axis=1)
    back_sum = lax.all_to_all(local_sum, "label", split_axis=0, concat_axis=0, tiled=True)
    exp_total = jnp.sum(from_slots(back_sum, picker).reshape(row_count, top_count), axis=1)
    normal = row_peak + jnp.log(exp_total)
    first_hit = jnp.arange(row_count * top_count, dtype=jnp.int32) % top_count == 0
    target_entry = jnp.where(first_hit, jnp.repeat(positive_offset, top_count) + 1, 0).astype(
        jnp.float32
    )
    norm_slots = to_slots(jnp.repeat(normal, top_count), picker)
    target_slots = to_slots(target_entry, picker)
    norm_here, target_here = (
        lax.all_to_all(norm_slots, "label", split_axis=0, concat_axis=0, tiled=True),
        lax.all_to_all(target_slots, "label", split_axis=0, concat_axis=0, tiled=True),
    )
    label_count = weights.shape[0]
    hit_label = jnp.arange(label_count, dtype=jnp.float32)[None, :] + 1.0 == target_here[:, None]
    probability = jnp.exp(scores - norm_here[:, None])
    coefficient = (probability - hit_label.astype(jnp.float32)).astype(jnp.bfloat16)
    positive_score = jnp.sum(jnp.where(hit_label, scores, 0.0), axis=1).astype(jnp.bfloat16)
    slot_grad = jnp.dot(coefficient, weights, preferred_element_type=jnp.float32).astype(
        jnp.bfloat16
    )
    back_grad, back_score = (
        lax.all_to_all(slot_grad, "label", split_axis=0, concat_axis=0, tiled=True),
        lax.all_to_all(positive_score, "label", split_axis=0, concat_axis=0, tiled=True),
    )
    query_grad = jnp.dot(dispatch, back_grad, preferred_element_type=jnp.float32).astype(
        jnp.bfloat16
    )
    entry_score = from_slots(back_score.astype(jnp.float32), picker).reshape(row_count, top_count)
    query_loss = normal - entry_score[:, 0]
    partial_sum = lax.dot_general(
        coefficient, arrived, (((0,), (0,)), ((), ())), preferred_element_type=jnp.float32
    )
    reduced = lax.psum_scatter(partial_sum, "dp", scatter_dimension=0, tiled=True)
    weight_grad = reduced.astype(jnp.bfloat16)
    return (query_loss, query_grad, weight_grad)


FAR = 1e30
NT = (((1,), (1,)), ((), ()))
TN = (((0,), (0,)), ((), ()))
ROOM = pltpu.CompilerParams(vmem_limit_bytes=20 * 1024 * 1024)


def cost(flops, size, exps=0):
    return pl.CostEstimate(flops=int(flops), bytes_accessed=int(size), transcendentals=int(exps))


def named(bits, shard):
    return (jnp.right_shift(bits, shard) & 1) == 1


def slabs(where, labels):
    me, lane = where[0], where[1]
    part = labels // 4
    for core in range(2):
        for side in range(2):
            for x in range(2):
                first = (me ^ side) * labels + ((2 * x + core) ^ lane) * part
                yield pl.ds((4 * core + 2 * side + x) * part, part), side, first


def pieces(part):
    unit = 2 * part // 20
    cuts, start = [], 0
    for size in CUTS:
        runs, here, size = [], 0, size * unit
        while here < size:
            x, row = divmod(start + here, part)
            runs.append((x, row, here, min(part - row, size - here)))
            here += runs[-1][3]
        cuts.append((size, runs))
        start += size
    return cuts


def pack(where, weights, counts, *outs):
    labels = weights.shape[0]
    part = labels // 4
    for out, (_, runs) in zip(outs, pieces(part)):
        for x, row, here, size in runs:
            base = pl.multiple_of((2 * x + where[1] % 2) * part + row, 16)
            out[pl.ds(here, size), :] = weights[pl.ds(base, size), :]
    size = pieces(part)[0][0]
    row = lax.broadcasted_iota(jnp.int32, (16, labels), 0)
    count = counts[...]
    high, low = jnp.right_shift(count, 6), count & 63
    digits = jnp.where(row == 0, high, jnp.where(row == 1, low, 0)).astype(jnp.float32)
    outs[0][pl.ds(size, 16), :] = jnp.zeros((16, outs[0].shape[1]), jnp.bfloat16)
    outs[0][pl.ds(size, 16), pl.ds(0, labels)] = digits.astype(jnp.bfloat16)


def score(held, q, logs, s_ref, e_ref):
    quarter = held.shape[0] // 4
    peaks = []
    for c in range(4):
        rows = pl.ds(c * quarter, quarter)
        s = lax.dot_general(held[rows, :], q, NT, preferred_element_type=jnp.float32) - logs[rows, :]
        s_ref[rows, :] = s
        peaks.append(jnp.max(s, axis=0, keepdims=True))
    peaks = [jnp.maximum(peaks[0], peaks[2]), jnp.maximum(peaks[1], peaks[3])]
    totals = []
    for c in range(4):
        rows = pl.ds(c * quarter, quarter)
        e = jnp.exp(s_ref[rows, :] - peaks[c % 2])
        e_ref[rows, :] = e
        totals.append(jnp.sum(e, axis=0, keepdims=True))
    return peaks[0], totals[0] + totals[2], peaks[1], totals[1] + totals[3]


def first_scores(cuts, where, qa, qb, weights, counts, *refs):
    count = len(cuts)
    near_pair, far_pair = refs[:count], refs[count : 2 * count]
    held, q, s_ref, e_ref, stats, logs, column = refs[2 * count :]
    lane = where[1]
    rows, labels = qa.shape[0], weights.shape[0]
    part = labels // 4
    q[pl.ds(0, rows), :] = qa[...]
    q[pl.ds(rows, rows), :] = qb[...]
    digits = near_pair[0][pl.ds(cuts[0][0], 16), :].astype(jnp.float32)[:, :labels]
    lines = (counts[...].astype(jnp.float32), digits[0:1] * 64.0 + digits[1:2])
    for side, line in enumerate(lines):
        column[...] = jnp.transpose(jnp.broadcast_to(jnp.log(line), (8, labels)))
        for core in range(2):
            for x in range(2):
                at = pl.ds((4 * core + 2 * side + x) * part, part)
                base = pl.multiple_of(((2 * x + core) ^ lane) * part, part)
                logs[at, :] = column[pl.ds(base, part), 0:1]
                if not side:
                    held[at, :] = weights[pl.ds(base, part), :]
    for core, got in enumerate((near_pair, far_pair)):
        for piece, (_, runs) in zip(got, cuts):
            for x, row, here, size in runs:
                first = pl.multiple_of((4 * core + 2 + (x ^ (lane // 2))) * part + row, 16)
                held[pl.ds(first, size), :] = piece[pl.ds(here, size), :]
    for i, v in enumerate(score(held, q[...], logs, s_ref, e_ref)):
        stats[2 * i : 2 * i + 1, :] = v[:, :rows]
        stats[2 * i + 1 : 2 * i + 2, :] = v[:, rows:]


def last_scores(qa, qb, held, logs, stats, meta, q, s_ref, e_ref, message):
    rows = qa.shape[0]
    q[pl.ds(0, rows), :] = qa[...]
    q[pl.ds(rows, rows), :] = qb[...]
    for i, v in enumerate(score(held, q[...], logs, s_ref, e_ref)):
        for k in range(2):
            at, to = 2 * i + k, 4 * i + A[k]
            message[to : to + 1, :] = stats[at : at + 1, :]
            to = 4 * i + B[k]
            message[to : to + 1, :] = v[:, k * rows : (k + 1) * rows]
    message[16:24, :] = meta[...]


def payload(term, lines, dtype):
    rows, width = term.shape
    lines = jnp.concatenate(lines + [jnp.zeros((8 - len(lines), rows), jnp.float32)], 0)
    lines = jnp.concatenate([lines, jnp.zeros((8, width - rows), jnp.float32)], 1)
    return jnp.concatenate([term, lines], 0).astype(dtype)


def block_lines(messages, me, j):
    bits = messages[j][16:17, :].astype(jnp.int32)
    pairs = []
    for k in range(4):
        for side in range(2):
            i = 8 * side + (j ^ k)
            here = named(bits, (me ^ (2 * k)) ^ side)
            pairs.append((here, messages[k][i : i + 1, :], messages[k][i + 4 : i + 5, :]))
    peak = functools.reduce(jnp.maximum, [jnp.where(n, m, LOW) for n, m, _ in pairs])
    total = sum(jnp.where(n, t * jnp.exp(jnp.where(n, m - peak, 0.0)), 0.0) for n, m, t in pairs)
    normal = peak + jnp.log(total)
    scales = [jnp.where(n, jnp.exp(jnp.where(n, m - normal, 0.0)), 0.0) for n, m, _ in pairs[:2]]
    return [normal] + scales + [messages[j][17:18, :].astype(jnp.int32)]


def pair_lines(messages, me, blocks):
    return [jnp.concatenate(v, 1) for v in zip(*(block_lines(messages, me, j) for j in blocks))]


def coefficients(blocks, labels, where, m0, m1, m2, m3, s_ref, e_ref, held, coef, last, lines):
    rows = m0.shape[1]
    normal, near, pair, target = pair_lines((m0, m1, m2, m3), where[0], blocks)
    index = lax.broadcasted_iota(jnp.int32, (labels // 4, 2 * rows), 0)
    positive = jnp.zeros((1, 2 * rows), jnp.float32)
    for at, side, first in slabs(where, labels):
        hot = index == target - first
        p = e_ref[at, :] * (pair if side else near)
        coef[at, :] = (p - jnp.where(hot, 1.0, 0.0)).astype(jnp.bfloat16)
        positive += jnp.sum(jnp.where(hot, s_ref[at, :], 0.0), axis=0, keepdims=True)
    lines[0:1, :] = positive
    lines[1:2, :] = normal
    term = lax.dot_general(coef[:, pl.ds(rows, rows)], held[...], TN, preferred_element_type=jnp.float32)
    last[...] = payload(term, [positive[:, rows:]], last.dtype)


def block_terms(coef, held, lines, out):
    rows = coef.shape[1] // 2
    term = lax.dot_general(coef[:, pl.ds(0, rows)], held[...], TN, preferred_element_type=jnp.float32)
    positive = lines[0:1, :rows].astype(jnp.bfloat16).astype(jnp.float32)
    if out.dtype == jnp.bfloat16:
        out[...] = payload(term, [positive], out.dtype)
    else:
        out[...] = payload(term.astype(jnp.bfloat16).astype(jnp.float32), [positive, lines[1:2, :rows]], out.dtype)


def label_terms(half, labels, where, m0, m1, m2, m3, e_a, e_b, qa, qb, out, coef):
    rows, part = m0.shape[1], labels // 4
    index = lax.broadcasted_iota(jnp.int32, (part, 2 * rows), 0)
    total = None
    for blocks, e_ref, q in ((A, e_a, qa), (B, e_b, qb)):
        _, near, pair, target = pair_lines((m0, m1, m2, m3), where[0], blocks)
        for i, (at, side, first) in enumerate(slabs(where, labels)):
            if i // 4 != half:
                continue
            hot = jnp.where(index == target - first, 1.0, 0.0)
            p = e_ref[at, :] * (pair if side else near)
            coef[pl.ds((i % 4) * part, part), :] = (p - hot).astype(jnp.bfloat16)
        term = jnp.dot(coef[...], q[...], preferred_element_type=jnp.float32)
        total = term if total is None else total + term
    out[...] = total.astype(out.dtype)


A, B = (1, 2), (0, 3)
CUTS = (7, 5, 4, 4)


def join(a, b, out):
    out[...] = (a[...].astype(jnp.float32) + b[...].astype(jnp.float32)).astype(out.dtype)


def add(a, b, out):
    out[...] = a[...] + b[...].astype(jnp.float32)


def finish(t, g, own, s0, s1, s2, loss, query_grad, weight_grad):
    f32 = jnp.float32
    rows = query_grad.shape[0]
    total = t[...] + g[...].astype(f32)
    query_grad[...] = total[:rows].astype(query_grad.dtype)
    loss[...] = total[rows + 1 : rows + 2, :rows] - total[rows : rows + 1, :rows]
    total = own[...] + sum(s[...].astype(f32) for s in (s0, s1, s2))
    weight_grad[...] = total.astype(weight_grad.dtype)


def dense_plan(queries, weights, counts, hits, positive_offset, cluster_shard):
    n = lax.axis_size("label")
    dp = lax.axis_size("dp")
    rows, width = queries.shape
    labels = weights.shape[0]
    part = labels // dp
    me = lax.axis_index("label")
    lane = lax.axis_index("dp")
    f32, bf16 = jnp.float32, jnp.bfloat16
    shape = jax.ShapeDtypeStruct

    def swap(x, k):
        return lax.ppermute(x, "label", [(i, i ^ (2 * k)) for i in range(n)])

    def pair(x):
        return lax.ppermute(x, "label", [(i, i ^ 1) for i in range(n)])

    def core(x):
        return lax.ppermute(x, "dp", [(i, i ^ 1) for i in range(dp)])

    def side(x):
        return lax.ppermute(x, "dp", [(i, i ^ 2) for i in range(dp)])

    def corner(x):
        return lax.ppermute(
            x, ("label", "dp"), [(i * dp + j, (i ^ 1) * dp + (j ^ 2)) for i in range(n) for j in range(dp)]
        )

    def call(kernel, outs, scalars, arrays, flops, size, scratch=(), name=None):
        return pl.pallas_call(
            kernel,
            out_shape=outs,
            in_specs=[pl.BlockSpec(memory_space=pltpu.SMEM)] * scalars
            + [pl.BlockSpec(memory_space=pltpu.VMEM)] * arrays,
            scratch_shapes=list(scratch),
            cost_estimate=cost(flops, size),
            compiler_params=ROOM,
            name=name,
        )

    where = jnp.stack([me, lane]).astype(jnp.int32)
    block_flops = 2 * (2 * labels) * (2 * rows) * width
    block_bytes = 2 * labels * (width * 2 + rows * 16)

    count_line = counts.reshape(1, labels)
    cuts = pieces(part)
    shapes = [shape((size + (0 if i else 16), width), bf16) for i, (size, _) in enumerate(cuts)]
    packed = call(pack, shapes, 1, 2, 0, labels * width * 2, (), "pack")(where, weights, count_line)
    near_pair = [pair(p) for p in packed]
    q2, q1 = swap(queries, 2), swap(queries, 1)

    match = hits[:, :, None] == jnp.arange(cluster_shard.shape[0], dtype=jnp.int32)[None, None, :]
    owner = jnp.sum(jnp.where(match, cluster_shard[None, None, :], 0), axis=2)
    bits = jnp.sum(jnp.left_shift(1, owner), axis=1)
    target = owner[:, 0] * labels + positive_offset
    meta = jnp.pad(jnp.stack([bits, target]).astype(f32), ((0, 6), (0, 0)))

    q3 = swap(q2, 1)
    far_pair = [core(p) for p in near_pair]

    scores = shape((2 * labels, 2 * rows), f32)
    held, qa, sa, ea, stats, logs = call(
        functools.partial(first_scores, cuts),
        (shape((2 * labels, width), bf16), shape((2 * rows, width), bf16), scores, scores, shape((8, rows), f32), shape((2 * labels, 1), f32)),
        1, 4 + 2 * len(cuts), block_flops, block_bytes, [pltpu.VMEM((labels, 8), f32)], "first_scores",
    )(where, q1, q2, weights, count_line, *near_pair, *far_pair)
    qb, sb, eb, message = call(
        last_scores,
        (shape((2 * rows, width), bf16), scores, scores, shape((24, rows), f32)),
        0, 6, block_flops, block_bytes, (), "last_scores",
    )(queries, q3, held, logs, stats, meta)

    m3, m2, m1 = swap(message, 3), swap(message, 2), swap(message, 1)
    term, line = shape((rows + 8, width), bf16), shape((2, 2 * rows), f32)

    def coefficient(blocks, s, e):
        return call(
            functools.partial(coefficients, blocks, labels),
            (shape((2 * labels, 2 * rows), bf16), term, line),
            1, 7, block_flops // 2, block_bytes, (), "coefficients",
        )(where, message, m1, m2, m3, s, e, held)

    def block_part(coef, lines, dtype):
        return call(block_terms, shape((rows + 8, width), dtype), 0, 3, block_flops // 2, block_bytes // 2, (), "block_terms")(coef, held, lines)

    def label_part(half, dtype):
        return call(
            functools.partial(label_terms, half, labels),
            shape((labels, width), dtype),
            1, 8, block_flops, block_bytes, [pltpu.VMEM((labels, 2 * rows), bf16)], "label_terms",
        )(where, message, m1, m2, m3, ea, eb, qa, qb)

    sent, kept = label_part(1, bf16), label_part(0, f32)
    arrived = core(sent)
    coef_b, t3, lines_b = coefficient(B, sb, eb)
    g3 = swap(t3, 1)
    coef_a, t2, lines_a = coefficient(A, sa, ea)
    t1 = block_part(coef_a, lines_a, bf16)
    t0 = block_part(coef_b, lines_b, f32)
    joined = call(join, term, 0, 2, 0, rows * width * 6, (), "join")(t2, g3)
    joined, t1 = lax.optimization_barrier((joined, t1))
    g1, g2 = swap(t1, 1), swap(joined, 2)
    summed = kept + arrived.astype(f32)
    sent = summed[part:].astype(bf16)
    s0, s1, s2 = side(sent[:part]), pair(sent[part : 2 * part]), corner(sent[2 * part :])
    both = call(add, shape((rows + 8, width), f32), 0, 2, 0, rows * width * 10, (), "add")(t0, g2)
    loss, query_grad, weight_grad = call(
        finish,
        (shape((1, rows), f32), shape((rows, width), bf16), shape((part, width), bf16)),
        0, 6, 0, 10 * (rows + part) * width, (), "finish",
    )(both, g1, summed[:part], s0, s1, s2)
    return loss[0], query_grad, weight_grad


def solution(mesh):
    n, dp = mesh.shape["label"], mesh.shape["dp"]

    def local(queries, weights, counts, hits, positive_offset, cluster_shard):
        rows, top = hits.shape
        args = (queries, weights, counts, hits, positive_offset, cluster_shard)
        dense = n == 8 and dp == 4 and weights.shape[0] % 640 == 0 and (n // 2) * rows <= 3 * rows * top // 2
        return dense_plan(*args) if dense else slot_plan(*args)

    return jax.shard_map(
        local,
        mesh=mesh,
        in_specs=(
            P(("label", "dp"), None),
            P("label", None),
            P("label"),
            P(("label", "dp"), None),
            P(("label", "dp")),
            P(),
        ),
        out_specs=(P(("label", "dp")), P(("label", "dp"), None), P(("label", "dp"), None)),
        check_vma=False,
    )
```

```python
import functools

import jax
import jax.numpy as jnp
from jax import lax
from jax.experimental import pallas as pl
from jax.experimental.pallas import tpu as pltpu
from jax.sharding import PartitionSpec as P

exact = lax.Precision.HIGHEST
LOW = -1e30


def from_slots(values, picker):
    return jnp.dot(picker, values, precision=exact)


def to_slots(values, picker):
    return jnp.dot(values, picker, precision=exact)


def slot_plan(queries, weights, counts, hits, positive_offset, cluster_shard):
    peer_count = lax.axis_size("label")
    row_count, top_count = hits.shape
    slot_count = 3 * row_count * top_count // 2
    slot_depth = slot_count // peer_count
    cluster_count = cluster_shard.shape[0]
    hit_flat = hits.reshape(-1)
    match_table = hit_flat[:, None] == jnp.arange(cluster_count, dtype=jnp.int32)[None, :]
    target_shard = jnp.sum(jnp.where(match_table, cluster_shard[None, :], 0), axis=1)
    owner_table = (
        target_shard[:, None] == jnp.arange(peer_count, dtype=jnp.int32)[None, :]
    ).astype(jnp.int32)
    position = jnp.sum((jnp.cumsum(owner_table, axis=0) - owner_table) * owner_table, axis=1)
    slot_of = target_shard * slot_depth + position
    picker_bool = slot_of[:, None] == jnp.arange(slot_count, dtype=jnp.int32)[None, :]
    picker = picker_bool.astype(jnp.float32)
    dispatch = jnp.sum(picker_bool.reshape(row_count, top_count, slot_count), axis=1).astype(
        jnp.bfloat16
    )
    outgoing = lax.dot_general(
        dispatch, queries, (((0,), (0,)), ((), ())), preferred_element_type=jnp.float32
    ).astype(jnp.bfloat16)
    arrived = lax.all_to_all(outgoing, "label", split_axis=0, concat_axis=0, tiled=True)
    log_count = jnp.log(counts.astype(jnp.float32))
    scores = (
        lax.dot_general(
            arrived, weights, (((1,), (1,)), ((), ())), preferred_element_type=jnp.float32
        )
        - log_count[None, :]
    )
    local_max = jnp.max(scores, axis=1)
    back_max = lax.all_to_all(local_max, "label", split_axis=0, concat_axis=0, tiled=True)
    row_peak = jnp.max(from_slots(back_max, picker).reshape(row_count, top_count), axis=1)
    peak_slots = to_slots(jnp.repeat(row_peak, top_count), picker)
    peak_here = lax.all_to_all(peak_slots, "label", split_axis=0, concat_axis=0, tiled=True)
    local_sum = jnp.sum(jnp.exp(scores - peak_here[:, None]), axis=1)
    back_sum = lax.all_to_all(local_sum, "label", split_axis=0, concat_axis=0, tiled=True)
    exp_total = jnp.sum(from_slots(back_sum, picker).reshape(row_count, top_count), axis=1)
    normal = row_peak + jnp.log(exp_total)
    first_hit = jnp.arange(row_count * top_count, dtype=jnp.int32) % top_count == 0
    target_entry = jnp.where(first_hit, jnp.repeat(positive_offset, top_count) + 1, 0).astype(
        jnp.float32
    )
    norm_slots = to_slots(jnp.repeat(normal, top_count), picker)
    target_slots = to_slots(target_entry, picker)
    norm_here, target_here = (
        lax.all_to_all(norm_slots, "label", split_axis=0, concat_axis=0, tiled=True),
        lax.all_to_all(target_slots, "label", split_axis=0, concat_axis=0, tiled=True),
    )
    label_count = weights.shape[0]
    hit_label = jnp.arange(label_count, dtype=jnp.float32)[None, :] + 1.0 == target_here[:, None]
    probability = jnp.exp(scores - norm_here[:, None])
    coefficient = (probability - hit_label.astype(jnp.float32)).astype(jnp.bfloat16)
    positive_score = jnp.sum(jnp.where(hit_label, scores, 0.0), axis=1).astype(jnp.bfloat16)
    slot_grad = jnp.dot(coefficient, weights, preferred_element_type=jnp.float32).astype(
        jnp.bfloat16
    )
    back_grad, back_score = (
        lax.all_to_all(slot_grad, "label", split_axis=0, concat_axis=0, tiled=True),
        lax.all_to_all(positive_score, "label", split_axis=0, concat_axis=0, tiled=True),
    )
    query_grad = jnp.dot(dispatch, back_grad, preferred_element_type=jnp.float32).astype(
        jnp.bfloat16
    )
    entry_score = from_slots(back_score.astype(jnp.float32), picker).reshape(row_count, top_count)
    query_loss = normal - entry_score[:, 0]
    partial_sum = lax.dot_general(
        coefficient, arrived, (((0,), (0,)), ((), ())), preferred_element_type=jnp.float32
    )
    reduced = lax.psum_scatter(partial_sum, "dp", scatter_dimension=0, tiled=True)
    weight_grad = reduced.astype(jnp.bfloat16)
    return (query_loss, query_grad, weight_grad)


FAR = 1e30
NT = (((1,), (1,)), ((), ()))
TN = (((0,), (0,)), ((), ()))
ROOM = pltpu.CompilerParams(vmem_limit_bytes=20 * 1024 * 1024)


def cost(flops, size, exps=0):
    return pl.CostEstimate(flops=int(flops), bytes_accessed=int(size), transcendentals=int(exps))


def named(bits, shard):
    return (jnp.right_shift(bits, shard) & 1) == 1


def slabs(where, labels):
    me, lane = where[0], where[1]
    part = labels // 4
    for core in range(2):
        for side in range(2):
            for x in range(2):
                first = (me ^ side) * labels + ((2 * x + core) ^ lane) * part
                yield pl.ds((4 * core + 2 * side + x) * part, part), side, first


def pieces(part):
    unit = 2 * part // 20
    cuts, start = [], 0
    for size in CUTS:
        runs, here, size = [], 0, size * unit
        while here < size:
            x, row = divmod(start + here, part)
            runs.append((x, row, here, min(part - row, size - here)))
            here += runs[-1][3]
        cuts.append((size, runs))
        start += size
    return cuts


def pack(where, weights, counts, *outs):
    labels = weights.shape[0]
    part = labels // 4
    for out, (_, runs) in zip(outs, pieces(part)):
        for x, row, here, size in runs:
            base = pl.multiple_of((2 * x + where[1] % 2) * part + row, 16)
            out[pl.ds(here, size), :] = weights[pl.ds(base, size), :]
    size = pieces(part)[0][0]
    row = lax.broadcasted_iota(jnp.int32, (16, labels), 0)
    count = counts[...]
    high, low = jnp.right_shift(count, 6), count & 63
    digits = jnp.where(row == 0, high, jnp.where(row == 1, low, 0)).astype(jnp.float32)
    outs[0][pl.ds(size, 16), :] = jnp.zeros((16, outs[0].shape[1]), jnp.bfloat16)
    outs[0][pl.ds(size, 16), pl.ds(0, labels)] = digits.astype(jnp.bfloat16)


def score(held, q, logs, s_ref, e_ref):
    quarter = held.shape[0] // 4
    peaks = []
    for c in range(4):
        rows = pl.ds(c * quarter, quarter)
        s = lax.dot_general(held[rows, :], q, NT, preferred_element_type=jnp.float32) - logs[rows, :]
        s_ref[rows, :] = s
        peaks.append(jnp.max(s, axis=0, keepdims=True))
    peaks = [jnp.maximum(peaks[0], peaks[2]), jnp.maximum(peaks[1], peaks[3])]
    totals = []
    for c in range(4):
        rows = pl.ds(c * quarter, quarter)
        e = jnp.exp(s_ref[rows, :] - peaks[c % 2])
        e_ref[rows, :] = e
        totals.append(jnp.sum(e, axis=0, keepdims=True))
    return peaks[0], totals[0] + totals[2], peaks[1], totals[1] + totals[3]


def first_scores(cuts, where, qa, qb, weights, counts, *refs):
    count = len(cuts)
    near_pair, far_pair = refs[:count], refs[count : 2 * count]
    held, q, s_ref, e_ref, stats, logs, column = refs[2 * count :]
    lane = where[1]
    rows, labels = qa.shape[0], weights.shape[0]
    part = labels // 4
    q[pl.ds(0, rows), :] = qa[...]
    q[pl.ds(rows, rows), :] = qb[...]
    digits = near_pair[0][pl.ds(cuts[0][0], 16), :].astype(jnp.float32)[:, :labels]
    lines = (counts[...].astype(jnp.float32), digits[0:1] * 64.0 + digits[1:2])
    for side, line in enumerate(lines):
        column[...] = jnp.transpose(jnp.broadcast_to(jnp.log(line), (8, labels)))
        for core in range(2):
            for x in range(2):
                at = pl.ds((4 * core + 2 * side + x) * part, part)
                base = pl.multiple_of(((2 * x + core) ^ lane) * part, part)
                logs[at, :] = column[pl.ds(base, part), 0:1]
                if not side:
                    held[at, :] = weights[pl.ds(base, part), :]
    for core, got in enumerate((near_pair, far_pair)):
        for piece, (_, runs) in zip(got, cuts):
            for x, row, here, size in runs:
                first = pl.multiple_of((4 * core + 2 + (x ^ (lane // 2))) * part + row, 16)
                held[pl.ds(first, size), :] = piece[pl.ds(here, size), :]
    for i, v in enumerate(score(held, q[...], logs, s_ref, e_ref)):
        stats[2 * i : 2 * i + 1, :] = v[:, :rows]
        stats[2 * i + 1 : 2 * i + 2, :] = v[:, rows:]


def last_scores(qa, qb, held, logs, stats, meta, q, s_ref, e_ref, message):
    rows = qa.shape[0]
    q[pl.ds(0, rows), :] = qa[...]
    q[pl.ds(rows, rows), :] = qb[...]
    for i, v in enumerate(score(held, q[...], logs, s_ref, e_ref)):
        for k in range(2):
            at, to = 2 * i + k, 4 * i + A[k]
            message[to : to + 1, :] = stats[at : at + 1, :]
            to = 4 * i + B[k]
            message[to : to + 1, :] = v[:, k * rows : (k + 1) * rows]
    message[16:24, :] = meta[...]


def payload(term, lines, dtype):
    rows, width = term.shape
    lines = jnp.concatenate(lines + [jnp.zeros((8 - len(lines), rows), jnp.float32)], 0)
    lines = jnp.concatenate([lines, jnp.zeros((8, width - rows), jnp.float32)], 1)
    return jnp.concatenate([term, lines], 0).astype(dtype)


def block_lines(messages, me, j):
    bits = messages[j][16:17, :].astype(jnp.int32)
    pairs = []
    for k in range(4):
        for side in range(2):
            i = 8 * side + (j ^ k)
            here = named(bits, (me ^ (2 * k)) ^ side)
            pairs.append((here, messages[k][i : i + 1, :], messages[k][i + 4 : i + 5, :]))
    peak = functools.reduce(jnp.maximum, [jnp.where(n, m, LOW) for n, m, _ in pairs])
    total = sum(jnp.where(n, t * jnp.exp(jnp.where(n, m - peak, 0.0)), 0.0) for n, m, t in pairs)
    normal = peak + jnp.log(total)
    scales = [jnp.where(n, jnp.exp(jnp.where(n, m - normal, 0.0)), 0.0) for n, m, _ in pairs[:2]]
    return [normal] + scales + [messages[j][17:18, :].astype(jnp.int32)]


def pair_lines(messages, me, blocks):
    return [jnp.concatenate(v, 1) for v in zip(*(block_lines(messages, me, j) for j in blocks))]


def coefficients(blocks, labels, where, m0, m1, m2, m3, s_ref, e_ref, held, coef, last, lines):
    rows = m0.shape[1]
    normal, near, pair, target = pair_lines((m0, m1, m2, m3), where[0], blocks)
    index = lax.broadcasted_iota(jnp.int32, (labels // 4, 2 * rows), 0)
    positive = jnp.zeros((1, 2 * rows), jnp.float32)
    for at, side, first in slabs(where, labels):
        hot = index == target - first
        p = e_ref[at, :] * (pair if side else near)
        coef[at, :] = (p - jnp.where(hot, 1.0, 0.0)).astype(jnp.bfloat16)
        positive += jnp.sum(jnp.where(hot, s_ref[at, :], 0.0), axis=0, keepdims=True)
    lines[0:1, :] = positive
    lines[1:2, :] = normal
    term = lax.dot_general(coef[:, pl.ds(rows, rows)], held[...], TN, preferred_element_type=jnp.float32)
    last[...] = payload(term, [positive[:, rows:]], last.dtype)


def block_terms(coef, held, lines, out):
    rows = coef.shape[1] // 2
    term = lax.dot_general(coef[:, pl.ds(0, rows)], held[...], TN, preferred_element_type=jnp.float32)
    positive = lines[0:1, :rows].astype(jnp.bfloat16).astype(jnp.float32)
    if out.dtype == jnp.bfloat16:
        out[...] = payload(term, [positive], out.dtype)
    else:
        out[...] = payload(term.astype(jnp.bfloat16).astype(jnp.float32), [positive, lines[1:2, :rows]], out.dtype)


def label_terms(half, labels, where, m0, m1, m2, m3, e_a, e_b, qa, qb, out, coef):
    rows, part = m0.shape[1], labels // 4
    index = lax.broadcasted_iota(jnp.int32, (part, 2 * rows), 0)
    total = None
    for blocks, e_ref, q in ((A, e_a, qa), (B, e_b, qb)):
        _, near, pair, target = pair_lines((m0, m1, m2, m3), where[0], blocks)
        for i, (at, side, first) in enumerate(slabs(where, labels)):
            if i // 4 != half:
                continue
            hot = jnp.where(index == target - first, 1.0, 0.0)
            p = e_ref[at, :] * (pair if side else near)
            coef[pl.ds((i % 4) * part, part), :] = (p - hot).astype(jnp.bfloat16)
        term = jnp.dot(coef[...], q[...], preferred_element_type=jnp.float32)
        total = term if total is None else total + term
    out[...] = total.astype(out.dtype)


A, B = (1, 2), (0, 3)
CUTS = (8, 6, 6)


def join(a, b, out):
    out[...] = (a[...].astype(jnp.float32) + b[...].astype(jnp.float32)).astype(out.dtype)


def add(a, b, out):
    out[...] = a[...] + b[...].astype(jnp.float32)


def finish(t, g, own, s0, s1, s2, loss, query_grad, weight_grad):
    f32 = jnp.float32
    rows = query_grad.shape[0]
    total = t[...] + g[...].astype(f32)
    query_grad[...] = total[:rows].astype(query_grad.dtype)
    loss[...] = total[rows + 1 : rows + 2, :rows] - total[rows : rows + 1, :rows]
    total = own[...] + sum(s[...].astype(f32) for s in (s0, s1, s2))
    weight_grad[...] = total.astype(weight_grad.dtype)


def dense_plan(queries, weights, counts, hits, positive_offset, cluster_shard):
    n = lax.axis_size("label")
    dp = lax.axis_size("dp")
    rows, width = queries.shape
    labels = weights.shape[0]
    part = labels // dp
    me = lax.axis_index("label")
    lane = lax.axis_index("dp")
    f32, bf16 = jnp.float32, jnp.bfloat16
    shape = jax.ShapeDtypeStruct

    def swap(x, k):
        return lax.ppermute(x, "label", [(i, i ^ (2 * k)) for i in range(n)])

    def pair(x):
        return lax.ppermute(x, "label", [(i, i ^ 1) for i in range(n)])

    def core(x):
        return lax.ppermute(x, "dp", [(i, i ^ 1) for i in range(dp)])

    def side(x):
        return lax.ppermute(x, "dp", [(i, i ^ 2) for i in range(dp)])

    def corner(x):
        return lax.ppermute(
            x, ("label", "dp"), [(i * dp + j, (i ^ 1) * dp + (j ^ 2)) for i in range(n) for j in range(dp)]
        )

    def call(kernel, outs, scalars, arrays, flops, size, scratch=(), name=None):
        return pl.pallas_call(
            kernel,
            out_shape=outs,
            in_specs=[pl.BlockSpec(memory_space=pltpu.SMEM)] * scalars
            + [pl.BlockSpec(memory_space=pltpu.VMEM)] * arrays,
            scratch_shapes=list(scratch),
            cost_estimate=cost(flops, size),
            compiler_params=ROOM,
            name=name,
        )

    where = jnp.stack([me, lane]).astype(jnp.int32)
    block_flops = 2 * (2 * labels) * (2 * rows) * width
    block_bytes = 2 * labels * (width * 2 + rows * 16)

    count_line = counts.reshape(1, labels)
    cuts = pieces(part)
    shapes = [shape((size + (0 if i else 16), width), bf16) for i, (size, _) in enumerate(cuts)]
    packed = call(pack, shapes, 1, 2, 0, labels * width * 2, (), "pack")(where, weights, count_line)
    near_pair = [pair(p) for p in packed]
    q2 = swap(queries, 2)
    q1 = swap(lax.optimization_barrier((queries, near_pair[1]))[0], 1)

    match = hits[:, :, None] == jnp.arange(cluster_shard.shape[0], dtype=jnp.int32)[None, None, :]
    owner = jnp.sum(jnp.where(match, cluster_shard[None, None, :], 0), axis=2)
    bits = jnp.sum(jnp.left_shift(1, owner), axis=1)
    target = owner[:, 0] * labels + positive_offset
    meta = jnp.pad(jnp.stack([bits, target]).astype(f32), ((0, 6), (0, 0)))

    q3 = swap(q2, 1)
    far_pair = [core(p) for p in near_pair]

    scores = shape((2 * labels, 2 * rows), f32)
    held, qa, sa, ea, stats, logs = call(
        functools.partial(first_scores, cuts),
        (shape((2 * labels, width), bf16), shape((2 * rows, width), bf16), scores, scores, shape((8, rows), f32), shape((2 * labels, 1), f32)),
        1, 4 + 2 * len(cuts), block_flops, block_bytes, [pltpu.VMEM((labels, 8), f32)], "first_scores",
    )(where, q1, q2, weights, count_line, *near_pair, *far_pair)
    qb, sb, eb, message = call(
        last_scores,
        (shape((2 * rows, width), bf16), scores, scores, shape((24, rows), f32)),
        0, 6, block_flops, block_bytes, (), "last_scores",
    )(queries, q3, held, logs, stats, meta)

    m3, m2, m1 = swap(message, 3), swap(message, 2), swap(message, 1)
    term, line = shape((rows + 8, width), bf16), shape((2, 2 * rows), f32)

    def coefficient(blocks, s, e):
        return call(
            functools.partial(coefficients, blocks, labels),
            (shape((2 * labels, 2 * rows), bf16), term, line),
            1, 7, block_flops // 2, block_bytes, (), "coefficients",
        )(where, message, m1, m2, m3, s, e, held)

    def block_part(coef, lines, dtype):
        return call(block_terms, shape((rows + 8, width), dtype), 0, 3, block_flops // 2, block_bytes // 2, (), "block_terms")(coef, held, lines)

    def label_part(half, dtype):
        return call(
            functools.partial(label_terms, half, labels),
            shape((labels, width), dtype),
            1, 8, block_flops, block_bytes, [pltpu.VMEM((labels, 2 * rows), bf16)], "label_terms",
        )(where, message, m1, m2, m3, ea, eb, qa, qb)

    sent, kept = label_part(1, bf16), label_part(0, f32)
    arrived = core(sent)
    coef_b, t3, lines_b = coefficient(B, sb, eb)
    g3 = swap(t3, 1)
    coef_a, t2, lines_a = coefficient(A, sa, ea)
    t1 = block_part(coef_a, lines_a, bf16)
    t0 = block_part(coef_b, lines_b, f32)
    joined = call(join, term, 0, 2, 0, rows * width * 6, (), "join")(t2, g3)
    joined, t1 = lax.optimization_barrier((joined, t1))
    g1, g2 = swap(t1, 1), swap(joined, 2)
    summed = kept + arrived.astype(f32)
    sent = summed[part:].astype(bf16)
    s0, s1, s2 = side(sent[:part]), pair(sent[part : 2 * part]), corner(sent[2 * part :])
    both = call(add, shape((rows + 8, width), f32), 0, 2, 0, rows * width * 10, (), "add")(t0, g2)
    loss, query_grad, weight_grad = call(
        finish,
        (shape((1, rows), f32), shape((rows, width), bf16), shape((part, width), bf16)),
        0, 6, 0, 10 * (rows + part) * width, (), "finish",
    )(both, g1, summed[:part], s0, s1, s2)
    return loss[0], query_grad, weight_grad


def solution(mesh):
    n, dp = mesh.shape["label"], mesh.shape["dp"]

    def local(queries, weights, counts, hits, positive_offset, cluster_shard):
        rows, top = hits.shape
        args = (queries, weights, counts, hits, positive_offset, cluster_shard)
        dense = n == 8 and dp == 4 and weights.shape[0] % 640 == 0 and (n // 2) * rows <= 3 * rows * top // 2
        return dense_plan(*args) if dense else slot_plan(*args)

    return jax.shard_map(
        local,
        mesh=mesh,
        in_specs=(
            P(("label", "dp"), None),
            P("label", None),
            P("label"),
            P(("label", "dp"), None),
            P(("label", "dp")),
            P(),
        ),
        out_specs=(P(("label", "dp")), P(("label", "dp"), None), P(("label", "dp"), None)),
        check_vma=False,
    )
```

```python
import functools

import jax
import jax.numpy as jnp
from jax import lax
from jax.experimental import pallas as pl
from jax.experimental.pallas import tpu as pltpu
from jax.sharding import PartitionSpec as P

exact = lax.Precision.HIGHEST
LOW = -1e30


def from_slots(values, picker):
    return jnp.dot(picker, values, precision=exact)


def to_slots(values, picker):
    return jnp.dot(values, picker, precision=exact)


def slot_plan(queries, weights, counts, hits, positive_offset, cluster_shard):
    peer_count = lax.axis_size("label")
    row_count, top_count = hits.shape
    slot_count = 3 * row_count * top_count // 2
    slot_depth = slot_count // peer_count
    cluster_count = cluster_shard.shape[0]
    hit_flat = hits.reshape(-1)
    match_table = hit_flat[:, None] == jnp.arange(cluster_count, dtype=jnp.int32)[None, :]
    target_shard = jnp.sum(jnp.where(match_table, cluster_shard[None, :], 0), axis=1)
    owner_table = (
        target_shard[:, None] == jnp.arange(peer_count, dtype=jnp.int32)[None, :]
    ).astype(jnp.int32)
    position = jnp.sum((jnp.cumsum(owner_table, axis=0) - owner_table) * owner_table, axis=1)
    slot_of = target_shard * slot_depth + position
    picker_bool = slot_of[:, None] == jnp.arange(slot_count, dtype=jnp.int32)[None, :]
    picker = picker_bool.astype(jnp.float32)
    dispatch = jnp.sum(picker_bool.reshape(row_count, top_count, slot_count), axis=1).astype(
        jnp.bfloat16
    )
    outgoing = lax.dot_general(
        dispatch, queries, (((0,), (0,)), ((), ())), preferred_element_type=jnp.float32
    ).astype(jnp.bfloat16)
    arrived = lax.all_to_all(outgoing, "label", split_axis=0, concat_axis=0, tiled=True)
    log_count = jnp.log(counts.astype(jnp.float32))
    scores = (
        lax.dot_general(
            arrived, weights, (((1,), (1,)), ((), ())), preferred_element_type=jnp.float32
        )
        - log_count[None, :]
    )
    local_max = jnp.max(scores, axis=1)
    back_max = lax.all_to_all(local_max, "label", split_axis=0, concat_axis=0, tiled=True)
    row_peak = jnp.max(from_slots(back_max, picker).reshape(row_count, top_count), axis=1)
    peak_slots = to_slots(jnp.repeat(row_peak, top_count), picker)
    peak_here = lax.all_to_all(peak_slots, "label", split_axis=0, concat_axis=0, tiled=True)
    local_sum = jnp.sum(jnp.exp(scores - peak_here[:, None]), axis=1)
    back_sum = lax.all_to_all(local_sum, "label", split_axis=0, concat_axis=0, tiled=True)
    exp_total = jnp.sum(from_slots(back_sum, picker).reshape(row_count, top_count), axis=1)
    normal = row_peak + jnp.log(exp_total)
    first_hit = jnp.arange(row_count * top_count, dtype=jnp.int32) % top_count == 0
    target_entry = jnp.where(first_hit, jnp.repeat(positive_offset, top_count) + 1, 0).astype(
        jnp.float32
    )
    norm_slots = to_slots(jnp.repeat(normal, top_count), picker)
    target_slots = to_slots(target_entry, picker)
    norm_here, target_here = (
        lax.all_to_all(norm_slots, "label", split_axis=0, concat_axis=0, tiled=True),
        lax.all_to_all(target_slots, "label", split_axis=0, concat_axis=0, tiled=True),
    )
    label_count = weights.shape[0]
    hit_label = jnp.arange(label_count, dtype=jnp.float32)[None, :] + 1.0 == target_here[:, None]
    probability = jnp.exp(scores - norm_here[:, None])
    coefficient = (probability - hit_label.astype(jnp.float32)).astype(jnp.bfloat16)
    positive_score = jnp.sum(jnp.where(hit_label, scores, 0.0), axis=1).astype(jnp.bfloat16)
    slot_grad = jnp.dot(coefficient, weights, preferred_element_type=jnp.float32).astype(
        jnp.bfloat16
    )
    back_grad, back_score = (
        lax.all_to_all(slot_grad, "label", split_axis=0, concat_axis=0, tiled=True),
        lax.all_to_all(positive_score, "label", split_axis=0, concat_axis=0, tiled=True),
    )
    query_grad = jnp.dot(dispatch, back_grad, preferred_element_type=jnp.float32).astype(
        jnp.bfloat16
    )
    entry_score = from_slots(back_score.astype(jnp.float32), picker).reshape(row_count, top_count)
    query_loss = normal - entry_score[:, 0]
    partial_sum = lax.dot_general(
        coefficient, arrived, (((0,), (0,)), ((), ())), preferred_element_type=jnp.float32
    )
    reduced = lax.psum_scatter(partial_sum, "dp", scatter_dimension=0, tiled=True)
    weight_grad = reduced.astype(jnp.bfloat16)
    return (query_loss, query_grad, weight_grad)


FAR = 1e30
A, B = (1, 2), (0, 3)
CUTS = (8, 6, 6)
NT = (((1,), (1,)), ((), ()))
TN = (((0,), (0,)), ((), ()))
ROOM = pltpu.CompilerParams(vmem_limit_bytes=20 * 1024 * 1024)


def cost(flops, size, exps=0):
    return pl.CostEstimate(flops=int(flops), bytes_accessed=int(size), transcendentals=int(exps))


def named(bits, shard):
    return (jnp.right_shift(bits, shard) & 1) == 1


def slabs(where, labels):
    me, lane = where[0], where[1]
    part = labels // 4
    for core in range(2):
        for side in range(2):
            for x in range(2):
                first = (me ^ side) * labels + ((2 * x + core) ^ lane) * part
                yield pl.ds((4 * core + 2 * side + x) * part, part), side, first


def pieces(part):
    unit = 2 * part // 20
    cuts, start = [], 0
    for size in CUTS:
        runs, here, size = [], 0, size * unit
        while here < size:
            x, row = divmod(start + here, part)
            runs.append((x, row, here, min(part - row, size - here)))
            here += runs[-1][3]
        cuts.append((size, runs))
        start += size
    return cuts


def pack(where, weights, counts, *outs):
    labels = weights.shape[0]
    part = labels // 4
    for out, (_, runs) in zip(outs, pieces(part)):
        for x, row, here, size in runs:
            base = pl.multiple_of((2 * x + where[1] % 2) * part + row, 16)
            out[pl.ds(here, size), :] = weights[pl.ds(base, size), :]
    size = pieces(part)[0][0]
    row = lax.broadcasted_iota(jnp.int32, (16, labels), 0)
    count = counts[...]
    high, low = jnp.right_shift(count, 6), count & 63
    digits = jnp.where(row == 0, high, jnp.where(row == 1, low, 0)).astype(jnp.float32)
    outs[0][pl.ds(size, 16), :] = jnp.zeros((16, outs[0].shape[1]), jnp.bfloat16)
    outs[0][pl.ds(size, 16), pl.ds(0, labels)] = digits.astype(jnp.bfloat16)


def score(held, q, logs, s_ref, e_ref):
    quarter = held.shape[0] // 4
    peaks = []
    for c in range(4):
        rows = pl.ds(c * quarter, quarter)
        s = lax.dot_general(held[rows, :], q, NT, preferred_element_type=jnp.float32) - logs[rows, :]
        s_ref[rows, :] = s
        peaks.append(jnp.max(s, axis=0, keepdims=True))
    peaks = [jnp.maximum(peaks[0], peaks[2]), jnp.maximum(peaks[1], peaks[3])]
    totals = []
    for c in range(4):
        rows = pl.ds(c * quarter, quarter)
        e = jnp.exp(s_ref[rows, :] - peaks[c % 2])
        e_ref[rows, :] = e
        totals.append(jnp.sum(e, axis=0, keepdims=True))
    return peaks[0], totals[0] + totals[2], peaks[1], totals[1] + totals[3]


def first_scores(cuts, where, qa, qb, weights, counts, *refs):
    count = len(cuts)
    near_pair, far_pair = refs[:count], refs[count : 2 * count]
    held, q, s_ref, e_ref, stats, logs, column = refs[2 * count :]
    lane = where[1]
    rows, labels = qa.shape[0], weights.shape[0]
    part = labels // 4
    q[pl.ds(0, rows), :] = qa[...]
    q[pl.ds(rows, rows), :] = qb[...]
    digits = near_pair[0][pl.ds(cuts[0][0], 16), :].astype(jnp.float32)[:, :labels]
    lines = (counts[...].astype(jnp.float32), digits[0:1] * 64.0 + digits[1:2])
    for side, line in enumerate(lines):
        column[...] = jnp.transpose(jnp.broadcast_to(jnp.log(line), (8, labels)))
        for core in range(2):
            for x in range(2):
                at = pl.ds((4 * core + 2 * side + x) * part, part)
                base = pl.multiple_of(((2 * x + core) ^ lane) * part, part)
                logs[at, :] = column[pl.ds(base, part), 0:1]
                if not side:
                    held[at, :] = weights[pl.ds(base, part), :]
    for core, got in enumerate((near_pair, far_pair)):
        for piece, (_, runs) in zip(got, cuts):
            for x, row, here, size in runs:
                first = pl.multiple_of((4 * core + 2 + (x ^ (lane // 2))) * part + row, 16)
                held[pl.ds(first, size), :] = piece[pl.ds(here, size), :]
    for i, v in enumerate(score(held, q[...], logs, s_ref, e_ref)):
        stats[2 * i : 2 * i + 1, :] = v[:, :rows]
        stats[2 * i + 1 : 2 * i + 2, :] = v[:, rows:]


def last_scores(qa, qb, held, logs, stats, meta, q, s_ref, e_ref, message):
    rows = qa.shape[0]
    q[pl.ds(0, rows), :] = qa[...]
    q[pl.ds(rows, rows), :] = qb[...]
    for i, v in enumerate(score(held, q[...], logs, s_ref, e_ref)):
        for k in range(2):
            at, to = 2 * i + k, 4 * i + A[k]
            message[to : to + 1, :] = stats[at : at + 1, :]
            to = 4 * i + B[k]
            message[to : to + 1, :] = v[:, k * rows : (k + 1) * rows]
    message[16:24, :] = meta[...]


def payload(term, lines, dtype):
    rows, width = term.shape
    lines = jnp.concatenate(lines + [jnp.zeros((8 - len(lines), rows), jnp.float32)], 0)
    lines = jnp.concatenate([lines, jnp.zeros((8, width - rows), jnp.float32)], 1)
    return jnp.concatenate([term, lines], 0).astype(dtype)


def block_lines(messages, me, j):
    bits = messages[j][16:17, :].astype(jnp.int32)
    pairs = []
    for k in range(4):
        for side in range(2):
            i = 8 * side + (j ^ k)
            here = named(bits, (me ^ (2 * k)) ^ side)
            pairs.append((here, messages[k][i : i + 1, :], messages[k][i + 4 : i + 5, :]))
    peak = functools.reduce(jnp.maximum, [jnp.where(n, m, LOW) for n, m, _ in pairs])
    total = sum(jnp.where(n, t * jnp.exp(jnp.where(n, m - peak, 0.0)), 0.0) for n, m, t in pairs)
    normal = peak + jnp.log(total)
    scales = [jnp.where(n, jnp.exp(jnp.where(n, m - normal, 0.0)), 0.0) for n, m, _ in pairs[:2]]
    return [normal] + scales + [messages[j][17:18, :].astype(jnp.int32)]


def pair_lines(messages, me, blocks):
    return [jnp.concatenate(v, 1) for v in zip(*(block_lines(messages, me, j) for j in blocks))]


def coef_dot(coefs, held, rows):
    half = held.shape[0] // 2
    return sum(
        lax.dot_general(c[:, rows], held[pl.ds(i * half, half), :], TN, preferred_element_type=jnp.float32)
        for i, c in enumerate(coefs)
    )


def slab_coefs(half, labels, where, lines, e_ref, coef, s_ref=None):
    _, near, pair, target = lines
    part, positive = labels // 4, jnp.zeros_like(near)
    index = lax.broadcasted_iota(jnp.int32, (part, target.shape[1]), 0)
    for i, (at, side, first) in enumerate(slabs(where, labels)):
        if i // 4 == half or s_ref is not None:
            hot = index == target - first
        if s_ref is not None:
            positive += jnp.sum(jnp.where(hot, s_ref[at, :], 0.0), axis=0, keepdims=True)
        if i // 4 == half:
            p = e_ref[at, :] * (pair if side else near)
            coef[pl.ds((i % 4) * part, part), :] = (p - jnp.where(hot, 1.0, 0.0)).astype(jnp.bfloat16)
    return positive


def send_terms(labels, where, m0, m1, m2, m3, e_a, e_b, qa, qb, out, far_a, far_b):
    messages = (m0, m1, m2, m3)
    slab_coefs(1, labels, where, pair_lines(messages, where[0], A), e_a, far_a)
    slab_coefs(1, labels, where, pair_lines(messages, where[0], B), e_b, far_b)
    total = jnp.dot(far_a[...], qa[...], preferred_element_type=jnp.float32)
    total += jnp.dot(far_b[...], qb[...], preferred_element_type=jnp.float32)
    out[...] = total.astype(out.dtype)


def keep_terms(labels, where, m0, m1, m2, m3, e_a, near_b, qa, qb, out, near_a):
    slab_coefs(0, labels, where, pair_lines((m0, m1, m2, m3), where[0], A), e_a, near_a)
    total = jnp.dot(near_a[...], qa[...], preferred_element_type=jnp.float32)
    out[...] = total + jnp.dot(near_b[...], qb[...], preferred_element_type=jnp.float32)


def far_block(labels, where, m0, m1, m2, m3, s_ref, e_ref, far, held, last, lines, near):
    rows = m0.shape[1]
    found = pair_lines((m0, m1, m2, m3), where[0], B)
    positive = slab_coefs(0, labels, where, found, e_ref, near, s_ref)
    lines[0:1, :] = positive
    lines[1:2, :] = found[0]
    term = coef_dot((near, far), held, pl.ds(rows, rows))
    last[...] = payload(term, [positive[:, rows:]], last.dtype)


def next_block(labels, where, m0, m1, m2, m3, s_ref, near, far, held, last, lines):
    rows = m0.shape[1]
    found = pair_lines((m0, m1, m2, m3), where[0], A)
    positive = slab_coefs(2, labels, where, found, None, None, s_ref)
    lines[0:1, :] = positive
    lines[1:2, :] = found[0]
    term = coef_dot((near, far), held, pl.ds(rows, rows))
    last[...] = payload(term, [positive[:, rows:]], last.dtype)


def first_terms(coef_near, coef_far, held, lines, out):
    rows = coef_near.shape[1] // 2
    term = coef_dot((coef_near, coef_far), held, pl.ds(0, rows))
    positive = lines[0:1, :rows].astype(jnp.bfloat16).astype(jnp.float32)
    if out.dtype == jnp.bfloat16:
        out[...] = payload(term, [positive], out.dtype)
    else:
        out[...] = payload(term.astype(jnp.bfloat16).astype(jnp.float32), [positive, lines[1:2, :rows]], out.dtype)


def join(a, b, out):
    out[...] = (a[...].astype(jnp.float32) + b[...].astype(jnp.float32)).astype(out.dtype)


def add(a, b, out):
    out[...] = a[...] + b[...].astype(jnp.float32)


def finish(t, g, own, s0, s1, s2, loss, query_grad, weight_grad):
    f32 = jnp.float32
    rows = query_grad.shape[0]
    total = t[...] + g[...].astype(f32)
    query_grad[...] = total[:rows].astype(query_grad.dtype)
    loss[...] = total[rows + 1 : rows + 2, :rows] - total[rows : rows + 1, :rows]
    total = own[...] + sum(s[...].astype(f32) for s in (s0, s1, s2))
    weight_grad[...] = total.astype(weight_grad.dtype)


def dense_plan(queries, weights, counts, hits, positive_offset, cluster_shard):
    n = lax.axis_size("label")
    dp = lax.axis_size("dp")
    rows, width = queries.shape
    labels = weights.shape[0]
    part = labels // dp
    me = lax.axis_index("label")
    lane = lax.axis_index("dp")
    f32, bf16 = jnp.float32, jnp.bfloat16
    shape = jax.ShapeDtypeStruct

    def swap(x, k):
        return lax.ppermute(x, "label", [(i, i ^ (2 * k)) for i in range(n)])

    def pair(x):
        return lax.ppermute(x, "label", [(i, i ^ 1) for i in range(n)])

    def core(x):
        return lax.ppermute(x, "dp", [(i, i ^ 1) for i in range(dp)])

    def side(x):
        return lax.ppermute(x, "dp", [(i, i ^ 2) for i in range(dp)])

    def corner(x):
        return lax.ppermute(
            x, ("label", "dp"), [(i * dp + j, (i ^ 1) * dp + (j ^ 2)) for i in range(n) for j in range(dp)]
        )

    def call(kernel, outs, scalars, arrays, flops, size, scratch=(), name=None):
        return pl.pallas_call(
            kernel,
            out_shape=outs,
            in_specs=[pl.BlockSpec(memory_space=pltpu.SMEM)] * scalars
            + [pl.BlockSpec(memory_space=pltpu.VMEM)] * arrays,
            scratch_shapes=list(scratch),
            cost_estimate=cost(flops, size),
            compiler_params=ROOM,
            name=name,
        )

    where = jnp.stack([me, lane]).astype(jnp.int32)
    block_flops = 2 * (2 * labels) * (2 * rows) * width
    block_bytes = 2 * labels * (width * 2 + rows * 16)

    count_line = counts.reshape(1, labels)
    cuts = pieces(part)
    shapes = [shape((size + (0 if i else 16), width), bf16) for i, (size, _) in enumerate(cuts)]
    packed = call(pack, shapes, 1, 2, 0, labels * width * 2, (), "pack")(where, weights, count_line)
    near_pair = [pair(p) for p in packed]
    q2 = swap(queries, 2)
    q1 = swap(lax.optimization_barrier((queries, near_pair[1]))[0], 1)

    match = hits[:, :, None] == jnp.arange(cluster_shard.shape[0], dtype=jnp.int32)[None, None, :]
    owner = jnp.sum(jnp.where(match, cluster_shard[None, None, :], 0), axis=2)
    bits = jnp.sum(jnp.left_shift(1, owner), axis=1)
    target = owner[:, 0] * labels + positive_offset
    meta = jnp.pad(jnp.stack([bits, target]).astype(f32), ((0, 6), (0, 0)))

    q3 = swap(q2, 1)
    far_pair = [core(p) for p in near_pair]

    scores = shape((2 * labels, 2 * rows), f32)
    held, qa, sa, ea, stats, logs = call(
        functools.partial(first_scores, cuts),
        (shape((2 * labels, width), bf16), shape((2 * rows, width), bf16), scores, scores, shape((8, rows), f32), shape((2 * labels, 1), f32)),
        1, 4 + 2 * len(cuts), block_flops, block_bytes, [pltpu.VMEM((labels, 8), f32)], "first_scores",
    )(where, q1, q2, weights, count_line, *near_pair, *far_pair)
    qb, sb, eb, message = call(
        last_scores,
        (shape((2 * rows, width), bf16), scores, scores, shape((24, rows), f32)),
        0, 6, block_flops, block_bytes, (), "last_scores",
    )(queries, q3, held, logs, stats, meta)

    m3, m2, m1 = swap(message, 3), swap(message, 2), swap(message, 1)
    term, line = shape((rows + 8, width), bf16), shape((2, 2 * rows), f32)

    coefs = shape((labels, 2 * rows), bf16)
    stated = (where, message, m1, m2, m3)

    def first_part(near, far, lines, dtype):
        return call(
            first_terms, shape((rows + 8, width), dtype), 0, 4, block_flops // 2, block_bytes // 2, (), "first_terms"
        )(near, far, held, lines)

    sent, far_a, far_b = call(
        functools.partial(send_terms, labels),
        (shape((labels, width), bf16), coefs, coefs),
        1, 8, block_flops, block_bytes, (), "send_terms",
    )(*stated, ea, eb, qa, qb)
    arrived = core(sent)
    t3, lines_b, near_b = call(
        functools.partial(far_block, labels), (term, line, coefs), 1, 8, block_flops // 2, block_bytes, (), "far_block"
    )(*stated, sb, eb, far_b, held)
    g3 = swap(t3, 1)
    kept, near_a = call(
        functools.partial(keep_terms, labels),
        (shape((labels, width), f32), coefs),
        1, 8, block_flops, block_bytes, (), "keep_terms",
    )(*stated, ea, near_b, qa, qb)
    t2, lines_a = call(
        functools.partial(next_block, labels), (term, line), 1, 8, block_flops // 2, block_bytes, (), "next_block"
    )(*stated, sa, near_a, far_a, held)
    t0 = first_part(near_b, far_b, lines_b, f32)
    joined = call(join, term, 0, 2, 0, rows * width * 6, (), "join")(t2, g3)
    joined, lines_a = lax.optimization_barrier((joined, lines_a))
    t1 = first_part(near_a, far_a, lines_a, bf16)
    g1, g2 = swap(t1, 1), swap(joined, 2)
    summed = kept + arrived.astype(f32)
    sent = summed[part:].astype(bf16)
    s0, s1, s2 = side(sent[:part]), pair(sent[part : 2 * part]), corner(sent[2 * part :])
    both = call(add, shape((rows + 8, width), f32), 0, 2, 0, rows * width * 10, (), "add")(t0, g2)
    loss, query_grad, weight_grad = call(
        finish,
        (shape((1, rows), f32), shape((rows, width), bf16), shape((part, width), bf16)),
        0, 6, 0, 10 * (rows + part) * width, (), "finish",
    )(both, g1, summed[:part], s0, s1, s2)
    return loss[0], query_grad, weight_grad


def solution(mesh):
    n, dp = mesh.shape["label"], mesh.shape["dp"]

    def local(queries, weights, counts, hits, positive_offset, cluster_shard):
        rows, top = hits.shape
        args = (queries, weights, counts, hits, positive_offset, cluster_shard)
        dense = n == 8 and dp == 4 and weights.shape[0] % 640 == 0 and (n // 2) * rows <= 3 * rows * top // 2
        return dense_plan(*args) if dense else slot_plan(*args)

    return jax.shard_map(
        local,
        mesh=mesh,
        in_specs=(
            P(("label", "dp"), None),
            P("label", None),
            P("label"),
            P(("label", "dp"), None),
            P(("label", "dp")),
            P(),
        ),
        out_specs=(P(("label", "dp")), P(("label", "dp"), None), P(("label", "dp"), None)),
        check_vma=False,
    )
```

```python
import functools

import jax
import jax.numpy as jnp
from jax import lax
from jax.experimental import pallas as pl
from jax.experimental.pallas import tpu as pltpu
from jax.sharding import PartitionSpec as P

exact = lax.Precision.HIGHEST
LOW = -1e30


def from_slots(values, picker):
    return jnp.dot(picker, values, precision=exact)


def to_slots(values, picker):
    return jnp.dot(values, picker, precision=exact)


def slot_plan(queries, weights, counts, hits, positive_offset, cluster_shard):
    peer_count = lax.axis_size("label")
    row_count, top_count = hits.shape
    slot_count = 3 * row_count * top_count // 2
    slot_depth = slot_count // peer_count
    cluster_count = cluster_shard.shape[0]
    hit_flat = hits.reshape(-1)
    match_table = hit_flat[:, None] == jnp.arange(cluster_count, dtype=jnp.int32)[None, :]
    target_shard = jnp.sum(jnp.where(match_table, cluster_shard[None, :], 0), axis=1)
    owner_table = (
        target_shard[:, None] == jnp.arange(peer_count, dtype=jnp.int32)[None, :]
    ).astype(jnp.int32)
    position = jnp.sum((jnp.cumsum(owner_table, axis=0) - owner_table) * owner_table, axis=1)
    slot_of = target_shard * slot_depth + position
    picker_bool = slot_of[:, None] == jnp.arange(slot_count, dtype=jnp.int32)[None, :]
    picker = picker_bool.astype(jnp.float32)
    dispatch = jnp.sum(picker_bool.reshape(row_count, top_count, slot_count), axis=1).astype(
        jnp.bfloat16
    )
    outgoing = lax.dot_general(
        dispatch, queries, (((0,), (0,)), ((), ())), preferred_element_type=jnp.float32
    ).astype(jnp.bfloat16)
    arrived = lax.all_to_all(outgoing, "label", split_axis=0, concat_axis=0, tiled=True)
    log_count = jnp.log(counts.astype(jnp.float32))
    scores = (
        lax.dot_general(
            arrived, weights, (((1,), (1,)), ((), ())), preferred_element_type=jnp.float32
        )
        - log_count[None, :]
    )
    local_max = jnp.max(scores, axis=1)
    back_max = lax.all_to_all(local_max, "label", split_axis=0, concat_axis=0, tiled=True)
    row_peak = jnp.max(from_slots(back_max, picker).reshape(row_count, top_count), axis=1)
    peak_slots = to_slots(jnp.repeat(row_peak, top_count), picker)
    peak_here = lax.all_to_all(peak_slots, "label", split_axis=0, concat_axis=0, tiled=True)
    local_sum = jnp.sum(jnp.exp(scores - peak_here[:, None]), axis=1)
    back_sum = lax.all_to_all(local_sum, "label", split_axis=0, concat_axis=0, tiled=True)
    exp_total = jnp.sum(from_slots(back_sum, picker).reshape(row_count, top_count), axis=1)
    normal = row_peak + jnp.log(exp_total)
    first_hit = jnp.arange(row_count * top_count, dtype=jnp.int32) % top_count == 0
    target_entry = jnp.where(first_hit, jnp.repeat(positive_offset, top_count) + 1, 0).astype(
        jnp.float32
    )
    norm_slots = to_slots(jnp.repeat(normal, top_count), picker)
    target_slots = to_slots(target_entry, picker)
    norm_here, target_here = (
        lax.all_to_all(norm_slots, "label", split_axis=0, concat_axis=0, tiled=True),
        lax.all_to_all(target_slots, "label", split_axis=0, concat_axis=0, tiled=True),
    )
    label_count = weights.shape[0]
    hit_label = jnp.arange(label_count, dtype=jnp.float32)[None, :] + 1.0 == target_here[:, None]
    probability = jnp.exp(scores - norm_here[:, None])
    coefficient = (probability - hit_label.astype(jnp.float32)).astype(jnp.bfloat16)
    positive_score = jnp.sum(jnp.where(hit_label, scores, 0.0), axis=1).astype(jnp.bfloat16)
    slot_grad = jnp.dot(coefficient, weights, preferred_element_type=jnp.float32).astype(
        jnp.bfloat16
    )
    back_grad, back_score = (
        lax.all_to_all(slot_grad, "label", split_axis=0, concat_axis=0, tiled=True),
        lax.all_to_all(positive_score, "label", split_axis=0, concat_axis=0, tiled=True),
    )
    query_grad = jnp.dot(dispatch, back_grad, preferred_element_type=jnp.float32).astype(
        jnp.bfloat16
    )
    entry_score = from_slots(back_score.astype(jnp.float32), picker).reshape(row_count, top_count)
    query_loss = normal - entry_score[:, 0]
    partial_sum = lax.dot_general(
        coefficient, arrived, (((0,), (0,)), ((), ())), preferred_element_type=jnp.float32
    )
    reduced = lax.psum_scatter(partial_sum, "dp", scatter_dimension=0, tiled=True)
    weight_grad = reduced.astype(jnp.bfloat16)
    return (query_loss, query_grad, weight_grad)


FAR = 1e30
A, B = (1, 2), (0, 3)
CUTS = (8, 6, 6)
NT = (((1,), (1,)), ((), ()))
TN = (((0,), (0,)), ((), ()))
ROOM = pltpu.CompilerParams(vmem_limit_bytes=20 * 1024 * 1024)


def cost(flops, size, exps=0):
    return pl.CostEstimate(flops=int(flops), bytes_accessed=int(size), transcendentals=int(exps))


def named(bits, shard):
    return (jnp.right_shift(bits, shard) & 1) == 1


def slabs(where, labels):
    me, lane = where[0], where[1]
    part = labels // 4
    for core in range(2):
        for side in range(2):
            for x in range(2):
                first = (me ^ side) * labels + ((2 * x + core) ^ lane) * part
                yield pl.ds((4 * core + 2 * side + x) * part, part), side, first


def pieces(part):
    unit = 2 * part // 20
    cuts, start = [], 0
    for size in CUTS:
        runs, here, size = [], 0, size * unit
        while here < size:
            x, row = divmod(start + here, part)
            runs.append((x, row, here, min(part - row, size - here)))
            here += runs[-1][3]
        cuts.append((size, runs))
        start += size
    return cuts


def pack(where, weights, counts, *outs):
    labels = weights.shape[0]
    part = labels // 4
    for out, (_, runs) in zip(outs, pieces(part)):
        for x, row, here, size in runs:
            base = pl.multiple_of((2 * x + where[1] % 2) * part + row, 16)
            out[pl.ds(here, size), :] = weights[pl.ds(base, size), :]
    size = pieces(part)[0][0]
    row = lax.broadcasted_iota(jnp.int32, (16, labels), 0)
    count = counts[...]
    high, low = jnp.right_shift(count, 6), count & 63
    digits = jnp.where(row == 0, high, jnp.where(row == 1, low, 0)).astype(jnp.float32)
    outs[0][pl.ds(size, 16), :] = jnp.zeros((16, outs[0].shape[1]), jnp.bfloat16)
    outs[0][pl.ds(size, 16), pl.ds(0, labels)] = digits.astype(jnp.bfloat16)


def score(held, q, logs, s_ref, e_ref):
    quarter = held.shape[0] // 4
    peaks = []
    for c in range(4):
        rows = pl.ds(c * quarter, quarter)
        s = lax.dot_general(held[rows, :], q, NT, preferred_element_type=jnp.float32) - logs[rows, :]
        s_ref[rows, :] = s
        peaks.append(jnp.max(s, axis=0, keepdims=True))
    peaks = [jnp.maximum(peaks[0], peaks[2]), jnp.maximum(peaks[1], peaks[3])]
    totals = []
    for c in range(4):
        rows = pl.ds(c * quarter, quarter)
        e = jnp.exp(s_ref[rows, :] - peaks[c % 2])
        e_ref[rows, :] = e
        totals.append(jnp.sum(e, axis=0, keepdims=True))
    return peaks[0], totals[0] + totals[2], peaks[1], totals[1] + totals[3]


def first_scores(cuts, where, qa, qb, weights, counts, *refs):
    count = len(cuts)
    near_pair, far_pair = refs[:count], refs[count : 2 * count]
    held, q, s_ref, e_ref, stats, logs, column = refs[2 * count :]
    lane = where[1]
    rows, labels = qa.shape[0], weights.shape[0]
    part = labels // 4
    q[pl.ds(0, rows), :] = qa[...]
    q[pl.ds(rows, rows), :] = qb[...]
    digits = near_pair[0][pl.ds(cuts[0][0], 16), :].astype(jnp.float32)[:, :labels]
    lines = (counts[...].astype(jnp.float32), digits[0:1] * 64.0 + digits[1:2])
    for side, line in enumerate(lines):
        column[...] = jnp.transpose(jnp.broadcast_to(jnp.log(line), (8, labels)))
        for core in range(2):
            for x in range(2):
                at = pl.ds((4 * core + 2 * side + x) * part, part)
                base = pl.multiple_of(((2 * x + core) ^ lane) * part, part)
                logs[at, :] = column[pl.ds(base, part), 0:1]
                if not side:
                    held[at, :] = weights[pl.ds(base, part), :]
    for core, got in enumerate((near_pair, far_pair)):
        for piece, (_, runs) in zip(got, cuts):
            for x, row, here, size in runs:
                first = pl.multiple_of((4 * core + 2 + (x ^ (lane // 2))) * part + row, 16)
                held[pl.ds(first, size), :] = piece[pl.ds(here, size), :]
    for i, v in enumerate(score(held, q[...], logs, s_ref, e_ref)):
        stats[2 * i : 2 * i + 1, :] = v[:, :rows]
        stats[2 * i + 1 : 2 * i + 2, :] = v[:, rows:]


def last_scores(qa, qb, held, logs, stats, meta, q, s_ref, e_ref, message):
    rows = qa.shape[0]
    q[pl.ds(0, rows), :] = qa[...]
    q[pl.ds(rows, rows), :] = qb[...]
    for i, v in enumerate(score(held, q[...], logs, s_ref, e_ref)):
        for k in range(2):
            at, to = 2 * i + k, 4 * i + A[k]
            message[to : to + 1, :] = stats[at : at + 1, :]
            to = 4 * i + B[k]
            message[to : to + 1, :] = v[:, k * rows : (k + 1) * rows]
    message[16:24, :] = meta[...]


def payload(term, lines, dtype):
    rows, width = term.shape
    lines = jnp.concatenate(lines + [jnp.zeros((8 - len(lines), rows), jnp.float32)], 0)
    lines = jnp.concatenate([lines, jnp.zeros((8, width - rows), jnp.float32)], 1)
    return jnp.concatenate([term, lines], 0).astype(dtype)


def block_lines(messages, me, j):
    bits = messages[j][16:17, :].astype(jnp.int32)
    pairs = []
    for k in range(4):
        for side in range(2):
            i = 8 * side + (j ^ k)
            here = named(bits, (me ^ (2 * k)) ^ side)
            pairs.append((here, messages[k][i : i + 1, :], messages[k][i + 4 : i + 5, :]))
    peak = functools.reduce(jnp.maximum, [jnp.where(n, m, LOW) for n, m, _ in pairs])
    total = sum(jnp.where(n, t * jnp.exp(jnp.where(n, m - peak, 0.0)), 0.0) for n, m, t in pairs)
    normal = peak + jnp.log(total)
    scales = [jnp.where(n, jnp.exp(jnp.where(n, m - normal, 0.0)), 0.0) for n, m, _ in pairs[:2]]
    return [normal] + scales + [messages[j][17:18, :].astype(jnp.int32)]


def pair_lines(messages, me, blocks):
    return [jnp.concatenate(v, 1) for v in zip(*(block_lines(messages, me, j) for j in blocks))]


def coef_dot(coefs, held, rows):
    half = held.shape[0] // 2
    return sum(
        lax.dot_general(c[:, rows], held[pl.ds(i * half, half), :], TN, preferred_element_type=jnp.float32)
        for i, c in enumerate(coefs)
    )


def slab_coefs(half, labels, where, lines, e_ref, coef, s_ref=None):
    _, near, pair, target = lines
    part, positive = labels // 4, jnp.zeros_like(near)
    index = lax.broadcasted_iota(jnp.int32, (part, target.shape[1]), 0)
    for i, (at, side, first) in enumerate(slabs(where, labels)):
        if i // 4 == half or s_ref is not None:
            hot = index == target - first
        if s_ref is not None:
            positive += jnp.sum(jnp.where(hot, s_ref[at, :], 0.0), axis=0, keepdims=True)
        if i // 4 == half:
            p = e_ref[at, :] * (pair if side else near)
            coef[pl.ds((i % 4) * part, part), :] = (p - jnp.where(hot, 1.0, 0.0)).astype(jnp.bfloat16)
    return positive


def send_terms(labels, where, m0, m1, m2, m3, e_a, e_b, qa, qb, out, far_a, far_b):
    messages = (m0, m1, m2, m3)
    slab_coefs(1, labels, where, pair_lines(messages, where[0], A), e_a, far_a)
    slab_coefs(1, labels, where, pair_lines(messages, where[0], B), e_b, far_b)
    total = jnp.dot(far_a[...], qa[...], preferred_element_type=jnp.float32)
    total += jnp.dot(far_b[...], qb[...], preferred_element_type=jnp.float32)
    out[...] = total.astype(out.dtype)


def keep_terms(labels, where, m0, m1, m2, m3, e_a, near_b, qa, qb, arrived, own, side, pair, corner, near_a):
    slab_coefs(0, labels, where, pair_lines((m0, m1, m2, m3), where[0], A), e_a, near_a)
    total = jnp.dot(near_a[...], qa[...], preferred_element_type=jnp.float32)
    total += jnp.dot(near_b[...], qb[...], preferred_element_type=jnp.float32)
    total += arrived[...].astype(jnp.float32)
    part = own.shape[0]
    for i, out in enumerate((own, side, pair, corner)):
        out[...] = total[i * part : (i + 1) * part].astype(out.dtype)


def far_block(labels, where, m0, m1, m2, m3, s_ref, e_ref, far, held, last, lines, near):
    rows = m0.shape[1]
    found = pair_lines((m0, m1, m2, m3), where[0], B)
    positive = slab_coefs(0, labels, where, found, e_ref, near, s_ref)
    lines[0:1, :] = positive
    lines[1:2, :] = found[0]
    term = coef_dot((near, far), held, pl.ds(rows, rows))
    last[...] = payload(term, [positive[:, rows:]], last.dtype)


def next_block(labels, where, m0, m1, m2, m3, s_ref, near, far, held, last, lines):
    rows = m0.shape[1]
    found = pair_lines((m0, m1, m2, m3), where[0], A)
    positive = slab_coefs(2, labels, where, found, None, None, s_ref)
    lines[0:1, :] = positive
    lines[1:2, :] = found[0]
    term = coef_dot((near, far), held, pl.ds(rows, rows))
    last[...] = payload(term, [positive[:, rows:]], last.dtype)


def first_terms(coef_near, coef_far, held, lines, out):
    rows = coef_near.shape[1] // 2
    term = coef_dot((coef_near, coef_far), held, pl.ds(0, rows))
    positive = lines[0:1, :rows].astype(jnp.bfloat16).astype(jnp.float32)
    if out.dtype == jnp.bfloat16:
        out[...] = payload(term, [positive], out.dtype)
    else:
        out[...] = payload(term.astype(jnp.bfloat16).astype(jnp.float32), [positive, lines[1:2, :rows]], out.dtype)


def join(a, b, out):
    out[...] = (a[...].astype(jnp.float32) + b[...].astype(jnp.float32)).astype(out.dtype)


def add(a, b, out):
    out[...] = a[...] + b[...].astype(jnp.float32)


def finish(t, g, own, s0, s1, s2, loss, query_grad, weight_grad):
    f32 = jnp.float32
    rows = query_grad.shape[0]
    total = t[...] + g[...].astype(f32)
    query_grad[...] = total[:rows].astype(query_grad.dtype)
    loss[...] = total[rows + 1 : rows + 2, :rows] - total[rows : rows + 1, :rows]
    total = own[...] + sum(s[...].astype(f32) for s in (s0, s1, s2))
    weight_grad[...] = total.astype(weight_grad.dtype)


def dense_plan(queries, weights, counts, hits, positive_offset, cluster_shard):
    n = lax.axis_size("label")
    dp = lax.axis_size("dp")
    rows, width = queries.shape
    labels = weights.shape[0]
    part = labels // dp
    me = lax.axis_index("label")
    lane = lax.axis_index("dp")
    f32, bf16 = jnp.float32, jnp.bfloat16
    shape = jax.ShapeDtypeStruct

    def swap(x, k):
        return lax.ppermute(x, "label", [(i, i ^ (2 * k)) for i in range(n)])

    def pair(x):
        return lax.ppermute(x, "label", [(i, i ^ 1) for i in range(n)])

    def core(x):
        return lax.ppermute(x, "dp", [(i, i ^ 1) for i in range(dp)])

    def side(x):
        return lax.ppermute(x, "dp", [(i, i ^ 2) for i in range(dp)])

    def corner(x):
        return lax.ppermute(
            x, ("label", "dp"), [(i * dp + j, (i ^ 1) * dp + (j ^ 2)) for i in range(n) for j in range(dp)]
        )

    def call(kernel, outs, scalars, arrays, flops, size, scratch=(), name=None):
        return pl.pallas_call(
            kernel,
            out_shape=outs,
            in_specs=[pl.BlockSpec(memory_space=pltpu.SMEM)] * scalars
            + [pl.BlockSpec(memory_space=pltpu.VMEM)] * arrays,
            scratch_shapes=list(scratch),
            cost_estimate=cost(flops, size),
            compiler_params=ROOM,
            name=name,
        )

    where = jnp.stack([me, lane]).astype(jnp.int32)
    block_flops = 2 * (2 * labels) * (2 * rows) * width
    block_bytes = 2 * labels * (width * 2 + rows * 16)

    count_line = counts.reshape(1, labels)
    cuts = pieces(part)
    shapes = [shape((size + (0 if i else 16), width), bf16) for i, (size, _) in enumerate(cuts)]
    packed = call(pack, shapes, 1, 2, 0, labels * width * 2, (), "pack")(where, weights, count_line)
    near_pair = [pair(p) for p in packed]
    q2 = swap(queries, 2)
    q1 = swap(lax.optimization_barrier((queries, near_pair[1]))[0], 1)

    match = hits[:, :, None] == jnp.arange(cluster_shard.shape[0], dtype=jnp.int32)[None, None, :]
    owner = jnp.sum(jnp.where(match, cluster_shard[None, None, :], 0), axis=2)
    bits = jnp.sum(jnp.left_shift(1, owner), axis=1)
    target = owner[:, 0] * labels + positive_offset
    meta = jnp.pad(jnp.stack([bits, target]).astype(f32), ((0, 6), (0, 0)))

    q3 = swap(q2, 1)
    far_pair = [core(p) for p in near_pair]

    scores = shape((2 * labels, 2 * rows), f32)
    held, qa, sa, ea, stats, logs = call(
        functools.partial(first_scores, cuts),
        (shape((2 * labels, width), bf16), shape((2 * rows, width), bf16), scores, scores, shape((8, rows), f32), shape((2 * labels, 1), f32)),
        1, 4 + 2 * len(cuts), block_flops, block_bytes, [pltpu.VMEM((labels, 8), f32)], "first_scores",
    )(where, q1, q2, weights, count_line, *near_pair, *far_pair)
    qb, sb, eb, message = call(
        last_scores,
        (shape((2 * rows, width), bf16), scores, scores, shape((24, rows), f32)),
        0, 6, block_flops, block_bytes, (), "last_scores",
    )(queries, q3, held, logs, stats, meta)

    m3, m2, m1 = swap(message, 3), swap(message, 2), swap(message, 1)
    term, line = shape((rows + 8, width), bf16), shape((2, 2 * rows), f32)

    coefs = shape((labels, 2 * rows), bf16)
    stated = (where, message, m1, m2, m3)

    def first_part(near, far, lines, dtype):
        return call(
            first_terms, shape((rows + 8, width), dtype), 0, 4, block_flops // 2, block_bytes // 2, (), "first_terms"
        )(near, far, held, lines)

    sent, far_a, far_b = call(
        functools.partial(send_terms, labels),
        (shape((labels, width), bf16), coefs, coefs),
        1, 8, block_flops, block_bytes, (), "send_terms",
    )(*stated, ea, eb, qa, qb)
    arrived = core(sent)
    t3, lines_b, near_b = call(
        functools.partial(far_block, labels), (term, line, coefs), 1, 8, block_flops // 2, block_bytes, (), "far_block"
    )(*stated, sb, eb, far_b, held)
    g3 = swap(t3, 1)
    portion = shape((part, width), bf16)
    own, to_side, to_pair, to_corner, near_a = call(
        functools.partial(keep_terms, labels),
        (shape((part, width), f32), portion, portion, portion, coefs),
        1, 9, block_flops, block_bytes, (), "keep_terms",
    )(*stated, ea, near_b, qa, qb, arrived)
    t2, lines_a = call(
        functools.partial(next_block, labels), (term, line), 1, 8, block_flops // 2, block_bytes, (), "next_block"
    )(*stated, sa, near_a, far_a, held)
    t0 = first_part(near_b, far_b, lines_b, f32)
    joined = call(join, term, 0, 2, 0, rows * width * 6, (), "join")(t2, g3)
    joined, lines_a = lax.optimization_barrier((joined, lines_a))
    t1 = first_part(near_a, far_a, lines_a, bf16)
    g1, g2 = swap(t1, 1), swap(joined, 2)
    s0, s1, s2 = side(to_side), pair(to_pair), corner(to_corner)
    both = call(add, shape((rows + 8, width), f32), 0, 2, 0, rows * width * 10, (), "add")(t0, g2)
    loss, query_grad, weight_grad = call(
        finish,
        (shape((1, rows), f32), shape((rows, width), bf16), shape((part, width), bf16)),
        0, 6, 0, 10 * (rows + part) * width, (), "finish",
    )(both, g1, own, s0, s1, s2)
    return loss[0], query_grad, weight_grad


def solution(mesh):
    n, dp = mesh.shape["label"], mesh.shape["dp"]

    def local(queries, weights, counts, hits, positive_offset, cluster_shard):
        rows, top = hits.shape
        args = (queries, weights, counts, hits, positive_offset, cluster_shard)
        dense = n == 8 and dp == 4 and weights.shape[0] % 640 == 0 and (n // 2) * rows <= 3 * rows * top // 2
        return dense_plan(*args) if dense else slot_plan(*args)

    return jax.shard_map(
        local,
        mesh=mesh,
        in_specs=(
            P(("label", "dp"), None),
            P("label", None),
            P("label"),
            P(("label", "dp"), None),
            P(("label", "dp")),
            P(),
        ),
        out_specs=(P(("label", "dp")), P(("label", "dp"), None), P(("label", "dp"), None)),
        check_vma=False,
    )
```

```python
import functools

import jax
import jax.numpy as jnp
from jax import lax
from jax.experimental import pallas as pl
from jax.experimental.pallas import tpu as pltpu
from jax.sharding import PartitionSpec as P

exact = lax.Precision.HIGHEST
LOW = -1e30


def from_slots(values, picker):
    return jnp.dot(picker, values, precision=exact)


def to_slots(values, picker):
    return jnp.dot(values, picker, precision=exact)


def slot_plan(queries, weights, counts, hits, positive_offset, cluster_shard):
    peer_count = lax.axis_size("label")
    row_count, top_count = hits.shape
    slot_count = 3 * row_count * top_count // 2
    slot_depth = slot_count // peer_count
    cluster_count = cluster_shard.shape[0]
    hit_flat = hits.reshape(-1)
    match_table = hit_flat[:, None] == jnp.arange(cluster_count, dtype=jnp.int32)[None, :]
    target_shard = jnp.sum(jnp.where(match_table, cluster_shard[None, :], 0), axis=1)
    owner_table = (
        target_shard[:, None] == jnp.arange(peer_count, dtype=jnp.int32)[None, :]
    ).astype(jnp.int32)
    position = jnp.sum((jnp.cumsum(owner_table, axis=0) - owner_table) * owner_table, axis=1)
    slot_of = target_shard * slot_depth + position
    picker_bool = slot_of[:, None] == jnp.arange(slot_count, dtype=jnp.int32)[None, :]
    picker = picker_bool.astype(jnp.float32)
    dispatch = jnp.sum(picker_bool.reshape(row_count, top_count, slot_count), axis=1).astype(
        jnp.bfloat16
    )
    outgoing = lax.dot_general(
        dispatch, queries, (((0,), (0,)), ((), ())), preferred_element_type=jnp.float32
    ).astype(jnp.bfloat16)
    arrived = lax.all_to_all(outgoing, "label", split_axis=0, concat_axis=0, tiled=True)
    log_count = jnp.log(counts.astype(jnp.float32))
    scores = (
        lax.dot_general(
            arrived, weights, (((1,), (1,)), ((), ())), preferred_element_type=jnp.float32
        )
        - log_count[None, :]
    )
    local_max = jnp.max(scores, axis=1)
    back_max = lax.all_to_all(local_max, "label", split_axis=0, concat_axis=0, tiled=True)
    row_peak = jnp.max(from_slots(back_max, picker).reshape(row_count, top_count), axis=1)
    peak_slots = to_slots(jnp.repeat(row_peak, top_count), picker)
    peak_here = lax.all_to_all(peak_slots, "label", split_axis=0, concat_axis=0, tiled=True)
    local_sum = jnp.sum(jnp.exp(scores - peak_here[:, None]), axis=1)
    back_sum = lax.all_to_all(local_sum, "label", split_axis=0, concat_axis=0, tiled=True)
    exp_total = jnp.sum(from_slots(back_sum, picker).reshape(row_count, top_count), axis=1)
    normal = row_peak + jnp.log(exp_total)
    first_hit = jnp.arange(row_count * top_count, dtype=jnp.int32) % top_count == 0
    target_entry = jnp.where(first_hit, jnp.repeat(positive_offset, top_count) + 1, 0).astype(
        jnp.float32
    )
    norm_slots = to_slots(jnp.repeat(normal, top_count), picker)
    target_slots = to_slots(target_entry, picker)
    norm_here, target_here = (
        lax.all_to_all(norm_slots, "label", split_axis=0, concat_axis=0, tiled=True),
        lax.all_to_all(target_slots, "label", split_axis=0, concat_axis=0, tiled=True),
    )
    label_count = weights.shape[0]
    hit_label = jnp.arange(label_count, dtype=jnp.float32)[None, :] + 1.0 == target_here[:, None]
    probability = jnp.exp(scores - norm_here[:, None])
    coefficient = (probability - hit_label.astype(jnp.float32)).astype(jnp.bfloat16)
    positive_score = jnp.sum(jnp.where(hit_label, scores, 0.0), axis=1).astype(jnp.bfloat16)
    slot_grad = jnp.dot(coefficient, weights, preferred_element_type=jnp.float32).astype(
        jnp.bfloat16
    )
    back_grad, back_score = (
        lax.all_to_all(slot_grad, "label", split_axis=0, concat_axis=0, tiled=True),
        lax.all_to_all(positive_score, "label", split_axis=0, concat_axis=0, tiled=True),
    )
    query_grad = jnp.dot(dispatch, back_grad, preferred_element_type=jnp.float32).astype(
        jnp.bfloat16
    )
    entry_score = from_slots(back_score.astype(jnp.float32), picker).reshape(row_count, top_count)
    query_loss = normal - entry_score[:, 0]
    partial_sum = lax.dot_general(
        coefficient, arrived, (((0,), (0,)), ((), ())), preferred_element_type=jnp.float32
    )
    reduced = lax.psum_scatter(partial_sum, "dp", scatter_dimension=0, tiled=True)
    weight_grad = reduced.astype(jnp.bfloat16)
    return (query_loss, query_grad, weight_grad)


FAR = 1e30
A, B = (1, 2), (0, 3)
CUTS = (8, 6, 6)
NT = (((1,), (1,)), ((), ()))
TN = (((0,), (0,)), ((), ()))
ROOM = pltpu.CompilerParams(vmem_limit_bytes=20 * 1024 * 1024)


def cost(flops, size, exps=0):
    return pl.CostEstimate(flops=int(flops), bytes_accessed=int(size), transcendentals=int(exps))


def named(bits, shard):
    return (jnp.right_shift(bits, shard) & 1) == 1


def slabs(where, labels):
    me, lane = where[0], where[1]
    part = labels // 4
    for core in range(2):
        for side in range(2):
            for x in range(2):
                first = (me ^ side) * labels + ((2 * x + core) ^ lane) * part
                yield pl.ds((4 * core + 2 * side + x) * part, part), side, first


def pieces(part):
    unit = 2 * part // 20
    cuts, start = [], 0
    for size in CUTS:
        runs, here, size = [], 0, size * unit
        while here < size:
            x, row = divmod(start + here, part)
            runs.append((x, row, here, min(part - row, size - here)))
            here += runs[-1][3]
        cuts.append((size, runs))
        start += size
    return cuts


def pack(where, weights, counts, *outs):
    labels = weights.shape[0]
    part = labels // 4
    for out, (_, runs) in zip(outs, pieces(part)):
        for x, row, here, size in runs:
            base = pl.multiple_of((2 * x + where[1] % 2) * part + row, 16)
            out[pl.ds(here, size), :] = weights[pl.ds(base, size), :]
    size = pieces(part)[0][0]
    row = lax.broadcasted_iota(jnp.int32, (16, labels), 0)
    count = counts[...]
    high, low = jnp.right_shift(count, 6), count & 63
    digits = jnp.where(row == 0, high, jnp.where(row == 1, low, 0)).astype(jnp.float32)
    outs[0][pl.ds(size, 16), :] = jnp.zeros((16, outs[0].shape[1]), jnp.bfloat16)
    outs[0][pl.ds(size, 16), pl.ds(0, labels)] = digits.astype(jnp.bfloat16)


def score(held, q, logs, s_ref, e_ref):
    quarter = held.shape[0] // 4
    peaks = []
    for c in range(4):
        rows = pl.ds(c * quarter, quarter)
        s = lax.dot_general(held[rows, :], q, NT, preferred_element_type=jnp.float32) - logs[rows, :]
        s_ref[rows, :] = s
        peaks.append(jnp.max(s, axis=0, keepdims=True))
    peaks = [jnp.maximum(peaks[0], peaks[2]), jnp.maximum(peaks[1], peaks[3])]
    totals = []
    for c in range(4):
        rows = pl.ds(c * quarter, quarter)
        e = jnp.exp(s_ref[rows, :] - peaks[c % 2])
        e_ref[rows, :] = e
        totals.append(jnp.sum(e, axis=0, keepdims=True))
    return peaks[0], totals[0] + totals[2], peaks[1], totals[1] + totals[3]


def first_scores(cuts, where, qa, qb, weights, counts, *refs):
    count = len(cuts)
    near_pair, far_pair = refs[:count], refs[count : 2 * count]
    held, q, s_ref, e_ref, stats, logs, column = refs[2 * count :]
    lane = where[1]
    rows, labels = qa.shape[0], weights.shape[0]
    part = labels // 4
    q[pl.ds(0, rows), :] = qa[...]
    q[pl.ds(rows, rows), :] = qb[...]
    digits = near_pair[0][pl.ds(cuts[0][0], 16), :].astype(jnp.float32)[:, :labels]
    lines = (counts[...].astype(jnp.float32), digits[0:1] * 64.0 + digits[1:2])
    for side, line in enumerate(lines):
        column[...] = jnp.transpose(jnp.broadcast_to(jnp.log(line), (8, labels)))
        for core in range(2):
            for x in range(2):
                at = pl.ds((4 * core + 2 * side + x) * part, part)
                base = pl.multiple_of(((2 * x + core) ^ lane) * part, part)
                logs[at, :] = column[pl.ds(base, part), 0:1]
                if not side:
                    held[at, :] = weights[pl.ds(base, part), :]
    for core, got in enumerate((near_pair, far_pair)):
        for piece, (_, runs) in zip(got, cuts):
            for x, row, here, size in runs:
                first = pl.multiple_of((4 * core + 2 + (x ^ (lane // 2))) * part + row, 16)
                held[pl.ds(first, size), :] = piece[pl.ds(here, size), :]
    for i, v in enumerate(score(held, q[...], logs, s_ref, e_ref)):
        stats[2 * i : 2 * i + 1, :] = v[:, :rows]
        stats[2 * i + 1 : 2 * i + 2, :] = v[:, rows:]


def last_scores(qa, qb, held, logs, stats, meta, q, s_ref, e_ref, message):
    rows = qa.shape[0]
    q[pl.ds(0, rows), :] = qa[...]
    q[pl.ds(rows, rows), :] = qb[...]
    for i, v in enumerate(score(held, q[...], logs, s_ref, e_ref)):
        for k in range(2):
            at, to = 2 * i + k, 4 * i + A[k]
            message[to : to + 1, :] = stats[at : at + 1, :]
            to = 4 * i + B[k]
            message[to : to + 1, :] = v[:, k * rows : (k + 1) * rows]
    message[16:24, :] = meta[...]


def payload(term, lines, dtype):
    rows, width = term.shape
    lines = jnp.concatenate(lines + [jnp.zeros((8 - len(lines), rows), jnp.float32)], 0)
    lines = jnp.concatenate([lines, jnp.zeros((8, width - rows), jnp.float32)], 1)
    return jnp.concatenate([term, lines], 0).astype(dtype)


def block_lines(messages, me, j):
    bits = messages[j][16:17, :].astype(jnp.int32)
    pairs = []
    for k in range(4):
        for side in range(2):
            i = 8 * side + (j ^ k)
            here = named(bits, (me ^ (2 * k)) ^ side)
            pairs.append((here, messages[k][i : i + 1, :], messages[k][i + 4 : i + 5, :]))
    peak = functools.reduce(jnp.maximum, [jnp.where(n, m, LOW) for n, m, _ in pairs])
    total = sum(jnp.where(n, t * jnp.exp(jnp.where(n, m - peak, 0.0)), 0.0) for n, m, t in pairs)
    normal = peak + jnp.log(total)
    scales = [jnp.where(n, jnp.exp(jnp.where(n, m - normal, 0.0)), 0.0) for n, m, _ in pairs[:2]]
    return [normal] + scales + [messages[j][17:18, :].astype(jnp.int32)]


def pair_lines(messages, me, blocks):
    return [jnp.concatenate(v, 1) for v in zip(*(block_lines(messages, me, j) for j in blocks))]


def coef_dot(coefs, held, rows):
    half = held.shape[0] // 2
    return sum(
        lax.dot_general(c[:, rows], held[pl.ds(i * half, half), :], TN, preferred_element_type=jnp.float32)
        for i, c in enumerate(coefs)
    )


def slab_coefs(half, labels, where, lines, e_ref, coef, s_ref=None):
    _, near, pair, target = lines
    part, positive = labels // 4, jnp.zeros_like(near)
    index = lax.broadcasted_iota(jnp.int32, (part, target.shape[1]), 0)
    for i, (at, side, first) in enumerate(slabs(where, labels)):
        if i // 4 == half or s_ref is not None:
            hot = index == target - first
        if s_ref is not None:
            positive += jnp.sum(jnp.where(hot, s_ref[at, :], 0.0), axis=0, keepdims=True)
        if i // 4 == half:
            p = e_ref[at, :] * (pair if side else near)
            coef[pl.ds((i % 4) * part, part), :] = (p - jnp.where(hot, 1.0, 0.0)).astype(jnp.bfloat16)
    return positive


def send_terms(labels, where, m0, m1, m2, m3, e_a, e_b, qa, qb, out, far_a, far_b):
    messages = (m0, m1, m2, m3)
    slab_coefs(1, labels, where, pair_lines(messages, where[0], A), e_a, far_a)
    slab_coefs(1, labels, where, pair_lines(messages, where[0], B), e_b, far_b)
    total = jnp.dot(far_a[...], qa[...], preferred_element_type=jnp.float32)
    total += jnp.dot(far_b[...], qb[...], preferred_element_type=jnp.float32)
    out[...] = total.astype(out.dtype)


def keep_terms(labels, where, m0, m1, m2, m3, e_a, near_b, qa, qb, arrived, own, side, pair, corner, near_a):
    slab_coefs(0, labels, where, pair_lines((m0, m1, m2, m3), where[0], A), e_a, near_a)
    total = jnp.dot(near_a[...], qa[...], preferred_element_type=jnp.float32)
    total += jnp.dot(near_b[...], qb[...], preferred_element_type=jnp.float32)
    total += arrived[...].astype(jnp.float32)
    part = own.shape[0]
    for i, out in enumerate((own, side, pair, corner)):
        out[...] = total[i * part : (i + 1) * part].astype(out.dtype)


def far_block(labels, where, m0, m1, m2, m3, s_ref, e_ref, far, held, last, lines, near):
    rows = m0.shape[1]
    found = pair_lines((m0, m1, m2, m3), where[0], B)
    positive = slab_coefs(0, labels, where, found, e_ref, near, s_ref)
    lines[0:1, :] = positive
    lines[1:2, :] = found[0]
    term = coef_dot((near, far), held, pl.ds(rows, rows))
    last[...] = payload(term, [positive[:, rows:]], last.dtype)


def next_block(labels, where, m0, m1, m2, m3, s_ref, near, far, held, last, lines):
    rows = m0.shape[1]
    found = pair_lines((m0, m1, m2, m3), where[0], A)
    positive = slab_coefs(2, labels, where, found, None, None, s_ref)
    lines[0:1, :] = positive
    lines[1:2, :] = found[0]
    term = coef_dot((near, far), held, pl.ds(rows, rows))
    last[...] = payload(term, [positive[:, rows:]], last.dtype)


def first_terms(coef_near, coef_far, held, lines, out):
    rows = coef_near.shape[1] // 2
    term = coef_dot((coef_near, coef_far), held, pl.ds(0, rows))
    positive = lines[0:1, :rows].astype(jnp.bfloat16).astype(jnp.float32)
    if out.dtype == jnp.bfloat16:
        out[...] = payload(term, [positive], out.dtype)
    else:
        out[...] = payload(term.astype(jnp.bfloat16).astype(jnp.float32), [positive, lines[1:2, :rows]], out.dtype)


def join(a, b, out):
    out[...] = (a[...].astype(jnp.float32) + b[...].astype(jnp.float32)).astype(out.dtype)


def add(a, b, out):
    out[...] = a[...] + b[...].astype(jnp.float32)


def finish_labels(own, s0, s1, s2, weight_grad):
    total = own[...] + sum(s[...].astype(jnp.float32) for s in (s0, s1, s2))
    weight_grad[...] = total.astype(weight_grad.dtype)


def finish_queries(t, g, loss, query_grad):
    rows = query_grad.shape[0]
    total = t[...] + g[...].astype(jnp.float32)
    query_grad[...] = total[:rows].astype(query_grad.dtype)
    loss[...] = total[rows + 1 : rows + 2, :rows] - total[rows : rows + 1, :rows]


def dense_plan(queries, weights, counts, hits, positive_offset, cluster_shard):
    n = lax.axis_size("label")
    dp = lax.axis_size("dp")
    rows, width = queries.shape
    labels = weights.shape[0]
    part = labels // dp
    me = lax.axis_index("label")
    lane = lax.axis_index("dp")
    f32, bf16 = jnp.float32, jnp.bfloat16
    shape = jax.ShapeDtypeStruct

    def swap(x, k):
        return lax.ppermute(x, "label", [(i, i ^ (2 * k)) for i in range(n)])

    def pair(x):
        return lax.ppermute(x, "label", [(i, i ^ 1) for i in range(n)])

    def core(x):
        return lax.ppermute(x, "dp", [(i, i ^ 1) for i in range(dp)])

    def side(x):
        return lax.ppermute(x, "dp", [(i, i ^ 2) for i in range(dp)])

    def corner(x):
        return lax.ppermute(
            x, ("label", "dp"), [(i * dp + j, (i ^ 1) * dp + (j ^ 2)) for i in range(n) for j in range(dp)]
        )

    def call(kernel, outs, scalars, arrays, flops, size, scratch=(), name=None):
        return pl.pallas_call(
            kernel,
            out_shape=outs,
            in_specs=[pl.BlockSpec(memory_space=pltpu.SMEM)] * scalars
            + [pl.BlockSpec(memory_space=pltpu.VMEM)] * arrays,
            scratch_shapes=list(scratch),
            cost_estimate=cost(flops, size),
            compiler_params=ROOM,
            name=name,
        )

    where = jnp.stack([me, lane]).astype(jnp.int32)
    block_flops = 2 * (2 * labels) * (2 * rows) * width
    block_bytes = 2 * labels * (width * 2 + rows * 16)

    count_line = counts.reshape(1, labels)
    cuts = pieces(part)
    shapes = [shape((size + (0 if i else 16), width), bf16) for i, (size, _) in enumerate(cuts)]
    packed = call(pack, shapes, 1, 2, 0, labels * width * 2, (), "pack")(where, weights, count_line)
    near_pair = [pair(p) for p in packed]
    q2 = swap(queries, 2)
    q1 = swap(lax.optimization_barrier((queries, near_pair[1]))[0], 1)

    match = hits[:, :, None] == jnp.arange(cluster_shard.shape[0], dtype=jnp.int32)[None, None, :]
    owner = jnp.sum(jnp.where(match, cluster_shard[None, None, :], 0), axis=2)
    bits = jnp.sum(jnp.left_shift(1, owner), axis=1)
    target = owner[:, 0] * labels + positive_offset
    meta = jnp.pad(jnp.stack([bits, target]).astype(f32), ((0, 6), (0, 0)))

    q3 = swap(q2, 1)
    far_pair = [core(p) for p in near_pair]

    scores = shape((2 * labels, 2 * rows), f32)
    held, qa, sa, ea, stats, logs = call(
        functools.partial(first_scores, cuts),
        (shape((2 * labels, width), bf16), shape((2 * rows, width), bf16), scores, scores, shape((8, rows), f32), shape((2 * labels, 1), f32)),
        1, 4 + 2 * len(cuts), block_flops, block_bytes, [pltpu.VMEM((labels, 8), f32)], "first_scores",
    )(where, q1, q2, weights, count_line, *near_pair, *far_pair)
    qb, sb, eb, message = call(
        last_scores,
        (shape((2 * rows, width), bf16), scores, scores, shape((24, rows), f32)),
        0, 6, block_flops, block_bytes, (), "last_scores",
    )(queries, q3, held, logs, stats, meta)

    m3, m2, m1 = swap(message, 3), swap(message, 2), swap(message, 1)
    term, line = shape((rows + 8, width), bf16), shape((2, 2 * rows), f32)

    coefs = shape((labels, 2 * rows), bf16)
    stated = (where, message, m1, m2, m3)

    def first_part(near, far, lines, dtype):
        return call(
            first_terms, shape((rows + 8, width), dtype), 0, 4, block_flops // 2, block_bytes // 2, (), "first_terms"
        )(near, far, held, lines)

    sent, far_a, far_b = call(
        functools.partial(send_terms, labels),
        (shape((labels, width), bf16), coefs, coefs),
        1, 8, block_flops, block_bytes, (), "send_terms",
    )(*stated, ea, eb, qa, qb)
    arrived = core(sent)
    t3, lines_b, near_b = call(
        functools.partial(far_block, labels), (term, line, coefs), 1, 8, block_flops // 2, block_bytes, (), "far_block"
    )(*stated, sb, eb, far_b, held)
    g3 = swap(t3, 1)
    portion = shape((part, width), bf16)
    own, to_side, to_pair, to_corner, near_a = call(
        functools.partial(keep_terms, labels),
        (shape((part, width), f32), portion, portion, portion, coefs),
        1, 9, block_flops, block_bytes, (), "keep_terms",
    )(*stated, ea, near_b, qa, qb, arrived)
    t2, lines_a = call(
        functools.partial(next_block, labels), (term, line), 1, 8, block_flops // 2, block_bytes, (), "next_block"
    )(*stated, sa, near_a, far_a, held)
    t0 = first_part(near_b, far_b, lines_b, f32)
    joined = call(join, term, 0, 2, 0, rows * width * 6, (), "join")(t2, g3)
    joined, lines_a = lax.optimization_barrier((joined, lines_a))
    t1 = first_part(near_a, far_a, lines_a, bf16)
    g1, g2 = swap(t1, 1), swap(joined, 2)
    s0, s1, s2 = side(to_side), pair(to_pair), corner(to_corner)
    weight_grad = call(
        finish_labels, shape((part, width), bf16), 0, 4, 0, 12 * part * width, (), "finish_labels"
    )(own, s0, s1, s2)
    g2, weight_grad = lax.optimization_barrier((g2, weight_grad))
    both = call(add, shape((rows + 8, width), f32), 0, 2, 0, rows * width * 10, (), "add")(t0, g2)
    loss, query_grad = call(
        finish_queries, (shape((1, rows), f32), shape((rows, width), bf16)), 0, 2, 0, 8 * rows * width, (), "finish_queries"
    )(both, g1)
    return loss[0], query_grad, weight_grad


def solution(mesh):
    n, dp = mesh.shape["label"], mesh.shape["dp"]

    def local(queries, weights, counts, hits, positive_offset, cluster_shard):
        rows, top = hits.shape
        args = (queries, weights, counts, hits, positive_offset, cluster_shard)
        dense = n == 8 and dp == 4 and weights.shape[0] % 640 == 0 and (n // 2) * rows <= 3 * rows * top // 2
        return dense_plan(*args) if dense else slot_plan(*args)

    return jax.shard_map(
        local,
        mesh=mesh,
        in_specs=(
            P(("label", "dp"), None),
            P("label", None),
            P("label"),
            P(("label", "dp"), None),
            P(("label", "dp")),
            P(),
        ),
        out_specs=(P(("label", "dp")), P(("label", "dp"), None), P(("label", "dp"), None)),
        check_vma=False,
    )
```
